32 devices in a mesh: groups: 2 (over x), blk: 16 (over z, y, core).
Axes of the slice: x: 2, y: 2, z: 4, core: 2. Of those that a mesh axis runs over, the one named last changes fastest.
Arguments:
- text_queries: bfloat16 [4096, 4096], P(('groups', 'blk')), parts along dimension 0, may hold values from -170 to 170
- image_states: bfloat16 [1536, 8192], P(('groups', 'blk')), parts along dimension 0, may hold values from -6 to 6
- kv_weight: bfloat16 [8192, 1024], P('blk'), may hold values from -0.1875 to 0.1875
- q_gain: float32 [128], replicated, may hold values from 0.25 to 1.75
- k_gain: float32 [128], replicated, may hold values from 0.25 to 1.75
- text_counts: int32 [6], P('groups'), parts along dimension 0, may hold values from 1 to 1024, 2048 in all
- image_counts: int32 [6], P('groups'), parts along dimension 0, may hold values from 96 to 384, as said below
Outputs:
- attended: bfloat16 [4096, 4096], P(('groups', 'blk')), parts along dimension 0
The draws below stay inside these ranges and needn't reach their ends.
There are 2 independent parts, one for each index of `groups`. The reference program is written for one: setup_inputs(seed, part) draws one part's arguments, and reference() takes and returns one part's arrays. A program takes and returns all parts, laid end to end along the dimension named above; an argument that names none is the same for every part. Nothing has to cross between parts.
Inputs may be any that keep to these rules, and one draw needn't show every extreme that they name: `text_counts`: they sum to 2048. `image_counts`: they sum to 768; the second image has exactly 384 tokens, the first and last are cut by the window.
All inputs are finite; a program needn't handle non-finite values.
Results may differ from the reference program's by a relative error of at most 0.0071.
Values may be sent and summed in bfloat16 or wider, within the bound.
A program may use at most 128 MiB of HBM per device.

```python
import math
import jax
import jax.numpy as jnp
import numpy as np
from jax import lax

D = 8192
HD = 128
QH = 32
KVH = 4
IMAGES = 3
TXT = 2048
IMG = 768


def draw_text_queries(key, part):
    key_base, key_column = jax.random.split(key, 2)
    base_values = jnp.clip(jax.random.normal(key_base, (TXT, QH * HD), jnp.float32), -4.0, 4.0)
    column_scale = jnp.exp(jax.random.uniform(key_column, (1, QH * HD), jnp.float32) * math.log(10.0))
    return (base_values * column_scale).astype(jnp.bfloat16)


def draw_image_counts(key, part):
    first = jax.random.randint(key, (), IMG // 8, 3 * IMG // 8 + 1, dtype=jnp.int32)
    middle = jnp.full((), IMG // 2, jnp.int32)
    last = IMG - IMG // 2 - first
    return jnp.stack([first, middle, last]).astype(jnp.int32)


def steps_of(key, extent, cuts, least, top_value):
    factor_of = 1.0
    for position, blocks in cuts:
        steps = jax.random.uniform(jax.random.fold_in(jax.random.fold_in(key, 6), position), (blocks,), jnp.float32, least / len(cuts), top_value / len(cuts))
        factor_of = factor_of * jnp.repeat(jnp.exp(steps), extent[position] // blocks).reshape((-1,) + (1,) * (len(extent) - 1 - position))
    return factor_of


def split_up(number_of, total, limit, lean):
    portions = [(1 << 20) // math.isqrt(grade ** lean) + 1 for grade in range(2, number_of + 1)]
    spare, counts = total - limit - (number_of - 1), [1] * (number_of - 1)
    while spare > 0:
        free = [i for i in range(number_of - 1) if counts[i] < limit]
        pool, budget = sum([portions[i] for i in free]), spare
        for i in free:
            extra = min(limit - counts[i], max(1, budget * portions[i] // pool), spare)
            counts[i] = counts[i] + extra
            spare = spare - extra
    return np.array([limit] + counts)


def ragged_sizes(own_key, number_of, total, limit, lean):
    if number_of == 2:
        one = jax.random.randint(own_key, (), max(1, total - limit), min(limit, total - 1) + 1)
        return jnp.stack([one, total - one])
    lengths = jnp.asarray(split_up(number_of, total, limit, lean), jnp.int32)
    pairs = (number_of - 1) // 2
    donor, taker = lengths[1:1 + 2 * pairs:2], lengths[2:2 + 2 * pairs:2]
    slack = jnp.minimum(donor - 1, limit - taker)
    moved = jax.random.randint(jax.random.fold_in(own_key, 1), (pairs,), 0, 1 << 20) % (slack + 1)
    lengths = lengths.at[1:1 + 2 * pairs:2].set(donor - moved).at[2:2 + 2 * pairs:2].set(taker + moved)
    return lengths[jax.random.permutation(jax.random.fold_in(own_key, 2), number_of)]


def noise(stream_key, shape, spread, reach, pieces=(), held_as=jnp.bfloat16):
    array = spread * jax.random.normal(stream_key, shape, jnp.float32)
    if pieces:
        array = array * steps_of(stream_key, shape, pieces, -0.22, 0.18)
    return jnp.clip(array, -reach, reach).astype(held_as)


def setup_inputs(seed: int = 0, part: int = 0) -> dict:
    seeds = jax.random.split(jax.random.key(seed), 8)
    part_splits = jax.random.split(jax.random.fold_in(seeds[7], part), 8)
    return {
        "text_queries": draw_text_queries(jax.random.fold_in(jax.random.fold_in(seeds[7], part), 71), part),
        "image_states": noise(part_splits[1], (IMG, D), 1.0, 6.0, ((0, 16),)),
        "kv_weight": noise(seeds[2], (D, 2 * KVH * HD), (D // 8) ** -0.5, 0.1875, ((0, 16),)),
        "q_gain": jnp.clip(1.0 + 0.15 * jax.random.normal(seeds[3], (HD,), jnp.float32), 0.25, 1.75),
        "k_gain": jnp.clip(1.0 + 0.15 * jax.random.normal(seeds[4], (HD,), jnp.float32), 0.25, 1.75),
        "text_counts": ragged_sizes(part_splits[5], IMAGES, TXT, TXT // 2, 2).astype(jnp.int32),
        "image_counts": draw_image_counts(jax.random.fold_in(jax.random.fold_in(seeds[7], part), 71), part),
    }


epsilon = 1e-05

def rms_norm(inputs, norm_gain):
    return inputs * lax.rsqrt(lax.optimization_barrier(jnp.mean(inputs * inputs, axis=-1, keepdims=True)) + epsilon) * norm_gain

def reference(text_queries, image_states, kv_weight, q_gain, k_gain, text_counts, image_counts):
    kv_width = KVH * HD
    group_size = QH // KVH
    projected = jnp.dot(image_states, kv_weight, preferred_element_type=jnp.float32)
    image_keys = rms_norm(projected[:, :kv_width].reshape(IMG, KVH, HD), k_gain).astype(jnp.bfloat16)
    image_values = projected[:, kv_width:].reshape(IMG, KVH, HD).astype(jnp.bfloat16)
    normed_queries = rms_norm(text_queries.astype(jnp.float32).reshape(TXT, QH, HD), q_gain).astype(jnp.bfloat16)
    normed_queries = normed_queries.reshape(TXT, KVH, group_size, HD)
    key_float = lax.optimization_barrier(image_keys).astype(jnp.float32)
    value_float = lax.optimization_barrier(image_values).astype(jnp.float32)
    query_float = lax.optimization_barrier(normed_queries).astype(jnp.float32)
    text_ends = jnp.cumsum(text_counts).astype(jnp.int32)
    image_ends = jnp.cumsum(image_counts).astype(jnp.int32)
    text_positions = jnp.arange(TXT, dtype=jnp.int32)
    image_positions = jnp.arange(IMG, dtype=jnp.int32)
    text_segment = lax.optimization_barrier(jnp.sum((text_ends[None, :] <= text_positions[:, None]).astype(jnp.int32), axis=1))
    image_owner = lax.optimization_barrier(jnp.sum((image_ends[None, :] <= image_positions[:, None]).astype(jnp.int32), axis=1))
    score_scale = 1.0 / math.sqrt(HD)
    row_block = math.gcd(TXT, 512)

    def attend_block(block_index):
        first_row = (block_index * row_block).astype(jnp.int32)
        query_rows = lax.dynamic_slice_in_dim(query_float, first_row, row_block, 0)
        segment = lax.dynamic_slice_in_dim(text_segment, first_row, row_block, 0)
        scores = jnp.einsum('tgrd,pgd->grtp', query_rows, key_float) * score_scale
        allowed = image_owner[None, :] <= segment[:, None]
        weights = jnp.where(allowed[None, None], jnp.exp(scores), 0.0)
        totals = lax.optimization_barrier(jnp.sum(weights, axis=-1))
        rounded = lax.optimization_barrier(weights.astype(jnp.bfloat16)).astype(jnp.float32)
        summed = jnp.einsum('grtp,pgd->tgrd', rounded, value_float)
        return (summed / jnp.transpose(totals, (2, 0, 1))[..., None]).astype(jnp.bfloat16)
    blocks = lax.map(attend_block, jnp.arange(TXT // row_block, dtype=jnp.int32))
    return blocks.reshape(TXT, QH * HD)
```

```python
import functools
import math

import jax
import jax.numpy as jnp
from jax import lax
from jax.experimental import pallas as pl
from jax.experimental.pallas import tpu as pltpu
from jax.sharding import PartitionSpec as P

epsilon = 1e-05
MESH = pl.DeviceIdType.MESH


def kernel(
    n,
    q_hbm,
    x_hbm,
    w_hbm,
    q_gain,
    k_gain,
    text_counts,
    image_counts,
    out,
    q_raw,
    q_normed,
    x_in,
    w,
    part_own,
    part_out,
    y_in,
    z_out,
    z_in,
    kv,
    bias,
    v_ones,
    local_sem,
    x_send,
    x_recv,
    w_send,
    w_recv,
    ry_send,
    ry_recv,
    rz_send,
    rz_recv,
    az_send,
    az_recv,
    ay_send,
    ay_recv,
    ac_send,
    ac_recv,
):
    f32, bf16 = jnp.float32, jnp.bfloat16
    me = lax.axis_index("blk")
    core = lax.rem(me, 2)
    chip = me // 2
    y = lax.rem(chip, 2)
    z = chip // 2
    depth = n // 4

    def device(z_, y_, core_):
        return {"blk": (z_ * 2 + y_) * 2 + core_}

    def copy(src, dst, send, recv, z_, y_, core_):
        return pltpu.make_async_remote_copy(
            src_ref=src,
            dst_ref=dst,
            send_sem=send,
            recv_sem=recv,
            device_id=device(z_, y_, core_),
            device_id_type=MESH,
        )

    rows, head_dim = x_hbm.shape[0], q_gain.shape[1]
    features = x_hbm.shape[1] * 2 // n
    w_rows, kv_cols = w_hbm.shape
    kv_width = kv_cols // 2
    kv_heads = kv_width // head_dim
    text_rows = q_hbm.shape[0]
    query_heads = q_hbm.shape[1] // head_dim
    group = query_heads // kv_heads
    keys = n * rows

    barrier = pltpu.get_barrier_semaphore()
    peers = []
    for dz in range(depth):
        for dy in range(2):
            if dz or dy:
                peers.append((lax.rem(z + dz, depth), lax.rem(y + dy, 2)))
    for pz, py in peers:
        pl.semaphore_signal(barrier, inc=1, device_id=device(pz, py, core), device_id_type=MESH)
    pl.semaphore_signal(barrier, inc=1, device_id=device(z, y, 1 - core), device_id_type=MESH)

    def x_block(pz, py):
        start = pl.multiple_of((pz * 2 + py) * features, features)
        return x_hbm.at[:, pl.ds(start, features)]

    own_w = pl.ds(pl.multiple_of(core * w_rows, w_rows), w_rows)
    x_local = pltpu.make_async_copy(x_block(z, y), x_in.at[y, z], local_sem.at[0])
    w_local = pltpu.make_async_copy(w_hbm, w.at[own_w], local_sem.at[1])
    q_local = pltpu.make_async_copy(q_hbm, q_raw, local_sem.at[2])
    x_local.start()
    w_local.start()
    q_local.start()

    pl.semaphore_wait(barrier, len(peers) + 1)

    sent = []
    w_copy = copy(w_hbm, w.at[own_w], w_send, w_recv, z, y, 1 - core)
    w_copy.start()
    for pz, py in peers:
        c = copy(
            x_block(pz, py), x_in.at[y, z], x_send.at[py, pz], x_recv.at[y, z], pz, py, core
        )
        c.start()
        sent.append(c)

    q_local.wait()
    for h in range(query_heads):
        v = q_raw[:, h * head_dim : (h + 1) * head_dim].astype(f32)
        mean = jnp.mean(v * v, axis=-1, keepdims=True)
        v = v * lax.rsqrt(mean + epsilon) * q_gain[...]
        at = (h % group) * text_rows
        q_normed[h // group, at : at + text_rows, :] = v.astype(bf16)

    t_pos = lax.broadcasted_iota(jnp.int32, (text_rows, keys), 0) + me * text_rows
    p_pos = lax.broadcasted_iota(jnp.int32, (text_rows, keys), 1)
    segment = jnp.zeros((text_rows, keys), jnp.int32)
    owner = jnp.zeros((text_rows, keys), jnp.int32)
    t_end, p_end = jnp.int32(0), jnp.int32(0)
    for j in range(text_counts.shape[0]):
        t_end = t_end + text_counts[j]
        p_end = p_end + image_counts[j]
        segment = segment + jnp.where(t_pos >= t_end, 1, 0)
        owner = owner + jnp.where(p_pos >= p_end, 1, 0)
    bias[...] = jnp.where(owner <= segment, 0.0, -1e30).astype(f32)
    v_ones[:, head_dim:] = jnp.ones((keys, head_dim), bf16)

    x_local.wait()
    w_local.wait()
    w_copy.wait_recv()

    def reduce_z(s):
        zt = lax.rem(z + depth - s, depth)
        copy(
            part_out.at[zt], y_in.at[zt], ry_send.at[zt], ry_recv.at[zt], z, 1 - y, core
        ).wait_recv()
        total = part_own[zt] + y_in[zt].astype(f32)
        z_out[zt] = total.astype(bf16)
        c = copy(z_out.at[zt], z_in.at[z], rz_send.at[zt], rz_recv.at[z], zt, y, core)
        c.start()
        sent.append(c)

    for s in range(depth):
        zs = lax.rem(z + depth - s, depth)
        for py in (y, 1 - y):
            if s == 0 and py is y:
                continue
            copy(
                x_in.at[py, zs], x_in.at[py, zs], x_send.at[py, zs], x_recv.at[py, zs], zs, py, core
            ).wait_recv()
        block = jnp.concatenate([x_in[y, zs], x_in[1 - y, zs]], axis=0)
        product = jnp.dot(block, w[...], preferred_element_type=f32)
        part_own[zs] = product[:rows]
        part_out[zs] = product[rows:].astype(bf16)
        c = copy(part_out.at[zs], y_in.at[zs], ry_send.at[zs], ry_recv.at[zs], z, 1 - y, core)
        c.start()
        sent.append(c)
        if s >= 2:
            reduce_z(s - 1)
    if depth >= 2:
        reduce_z(depth - 1)

    copy(part_out.at[z], y_in.at[z], ry_send.at[z], ry_recv.at[z], z, 1 - y, core).wait_recv()
    total = part_own[z] + y_in[z].astype(f32)
    for s in range(1, depth):
        zs = lax.rem(z + depth - s, depth)
        copy(z_out.at[zs], z_in.at[zs], rz_send.at[zs], rz_recv.at[zs], zs, y, core).wait_recv()
        total = total + z_in[zs].astype(f32)
    for g in range(kv_heads):
        at = slice(g * head_dim, (g + 1) * head_dim)
        v = total[:, at]
        mean = jnp.mean(v * v, axis=-1, keepdims=True)
        kv[me, :, at] = (v * lax.rsqrt(mean + epsilon) * k_gain[...]).astype(bf16)
    kv[me, :, kv_width:] = total[:, kv_width:].astype(bf16)

    def index(z_, y_, core_):
        return (z_ * 2 + y_) * 2 + core_

    def to_y(zb):
        block = kv.at[index(zb, y, core)]
        return copy(block, block, ay_send.at[zb], ay_recv.at[zb], z, 1 - y, core)

    def to_core(zb, yb):
        block = kv.at[index(zb, yb, core)]
        return copy(block, block, ac_send.at[yb, zb], ac_recv.at[yb, zb], z, y, 1 - core)

    for s in range(1, depth):
        zt = lax.rem(z + s, depth)
        c = copy(kv.at[me], kv.at[me], az_send.at[zt], az_recv.at[z], zt, y, core)
        c.start()
        sent.append(c)
    for c in (to_y(z), to_core(z, y)):
        c.start()
        sent.append(c)
    for s in range(1, depth):
        zs = lax.rem(z + depth - s, depth)
        block = kv.at[index(zs, y, core)]
        copy(block, block, az_send.at[zs], az_recv.at[zs], zs, y, core).wait_recv()
        for c in (to_y(zs), to_core(zs, y)):
            c.start()
            sent.append(c)
    for s in range(depth):
        zs = lax.rem(z + depth - s, depth)
        block = kv.at[index(zs, 1 - y, core)]
        copy(block, block, ay_send.at[zs], ay_recv.at[zs], z, 1 - y, core).wait_recv()
        c = to_core(zs, 1 - y)
        c.start()
        sent.append(c)
    for zs in range(depth):
        for yb in range(2):
            block = kv.at[index(zs, yb, 1 - core)]
            copy(
                block, block, ac_send.at[yb, zs], ac_recv.at[yb, zs], z, y, 1 - core
            ).wait_recv()

    scale = math.log2(math.e) / math.sqrt(head_dim)
    pair = 2 if group % 2 == 0 else 1
    tile = pair * text_rows

    @pl.loop(0, kv_heads)
    def _(g):
        k_at = pl.ds(pl.multiple_of(g * head_dim, head_dim), head_dim)
        v_at = pl.ds(pl.multiple_of(kv_width + g * head_dim, head_dim), head_dim)
        v_ones[:, :head_dim] = kv[:, :, v_at].reshape(keys, head_dim)
        key_block = kv[:, :, k_at].reshape(keys, head_dim)
        for t in range(group // pair):
            q = q_normed[g, t * tile : (t + 1) * tile, :]
            scores = lax.dot_general(
                q, key_block, (((1,), (1,)), ((), ())), preferred_element_type=f32
            )
            scores = scores.reshape(pair, text_rows, keys) * scale + bias[...][None]
            weights = jnp.exp2(scores).astype(bf16).reshape(tile, keys)
            sums = jnp.dot(weights, v_ones[...], preferred_element_type=f32)
            result = (sums[:, :head_dim] / sums[:, head_dim:]).astype(bf16)
            for i in range(pair):
                at = pl.multiple_of((g * group + t * pair + i) * head_dim, head_dim)
                out[:, pl.ds(at, head_dim)] = result[i * text_rows : (i + 1) * text_rows]

    w_copy.wait_send()
    for c in sent:
        c.wait_send()


def body(n, text_queries, image_states, kv_weight, q_gain, k_gain, text_counts, image_counts):
    f32, bf16 = jnp.float32, jnp.bfloat16
    rows = image_states.shape[0]
    features = image_states.shape[1] * 2 // n
    w_rows, kv_cols = kv_weight.shape
    text_rows, q_cols = text_queries.shape
    head_dim = q_gain.shape[0]
    kv_heads = kv_cols // 2 // head_dim
    group = q_cols // head_dim // kv_heads
    depth = n // 4
    keys = n * rows
    vmem = pl.BlockSpec(memory_space=pltpu.VMEM)
    smem = pl.BlockSpec(memory_space=pltpu.SMEM)
    anywhere = pl.BlockSpec(memory_space=pl.ANY)
    dma = pltpu.SemaphoreType.DMA
    return pl.pallas_call(
        functools.partial(kernel, n),
        out_shape=jax.ShapeDtypeStruct((text_rows, q_cols), bf16),
        in_specs=[anywhere, anywhere, anywhere, vmem, vmem, smem, smem],
        out_specs=vmem,
        scratch_shapes=[
            pltpu.VMEM((text_rows, q_cols), bf16),
            pltpu.VMEM((kv_heads, group * text_rows, head_dim), bf16),
            pltpu.VMEM((2, depth, rows, features), bf16),
            pltpu.VMEM((2 * w_rows, kv_cols), bf16),
            pltpu.VMEM((depth, rows, kv_cols), f32),
            pltpu.VMEM((depth, rows, kv_cols), bf16),
            pltpu.VMEM((depth, rows, kv_cols), bf16),
            pltpu.VMEM((depth, rows, kv_cols), bf16),
            pltpu.VMEM((depth, rows, kv_cols), bf16),
            pltpu.VMEM((n, rows, kv_cols), bf16),
            pltpu.VMEM((text_rows, keys), f32),
            pltpu.VMEM((keys, 2 * head_dim), bf16),
            dma((3,)),
            dma((2, depth)),
            dma((2, depth)),
            dma,
            dma,
            dma((depth,)),
            dma((depth,)),
            dma((depth,)),
            dma((depth,)),
            dma((depth,)),
            dma((depth,)),
            dma((depth,)),
            dma((depth,)),
            dma((2, depth)),
            dma((2, depth)),
        ],
        compiler_params=pltpu.CompilerParams(
            collective_id=0, has_side_effects=True, vmem_limit_bytes=48 << 20
        ),
    )(
        text_queries,
        image_states,
        kv_weight,
        q_gain.reshape(1, head_dim),
        k_gain.reshape(1, head_dim),
        text_counts,
        image_counts,
    )


def solution(mesh):
    placed = (
        P(("groups", "blk"), None),
        P(("groups", "blk"), None),
        P("blk", None),
        P(),
        P(),
        P("groups"),
        P("groups"),
    )
    return jax.shard_map(
        functools.partial(body, mesh.shape["blk"]),
        mesh=mesh,
        in_specs=placed,
        out_specs=P(("groups", "blk"), None),
        check_vma=False,
    )
```

```python
import functools
import math

import jax
import jax.numpy as jnp
from jax import lax
from jax.experimental import pallas as pl
from jax.experimental.pallas import tpu as pltpu
from jax.sharding import PartitionSpec as P

epsilon = 1e-05
MESH = pl.DeviceIdType.MESH


def kernel(
    n,
    q_hbm,
    x_hbm,
    w_hbm,
    q_gain,
    k_gain,
    text_counts,
    image_counts,
    out,
    q_raw,
    q_normed,
    x_in,
    w,
    part_own,
    part_out,
    y_in,
    z_out,
    z_in,
    kv,
    bias,
    sums,
    local_sem,
    xl_sem,
    x_send,
    x_recv,
    w_send,
    w_recv,
    ry_send,
    ry_recv,
    rz_send,
    rz_recv,
    az_send,
    az_recv,
    ay_send,
    ay_recv,
    ac_send,
    ac_recv,
):
    f32, bf16 = jnp.float32, jnp.bfloat16
    me = lax.axis_index("blk")
    core = lax.rem(me, 2)
    chip = me // 2
    y = lax.rem(chip, 2)
    z = chip // 2
    depth = n // 4

    def index(z_, y_, core_):
        return (z_ * 2 + y_) * 2 + core_

    def device(z_, y_, core_):
        return {"blk": index(z_, y_, core_)}

    def copy(src, dst, send, recv, z_, y_, core_):
        return pltpu.make_async_remote_copy(
            src_ref=src,
            dst_ref=dst,
            send_sem=send,
            recv_sem=recv,
            device_id=device(z_, y_, core_),
            device_id_type=MESH,
        )

    chunks, _, _, part, features = x_in.shape
    rows, head_dim = x_hbm.shape[0], q_gain.shape[1]
    w_rows, kv_cols = w_hbm.shape
    kv_width = kv_cols // 2
    kv_heads = kv_width // head_dim
    text_rows = q_hbm.shape[0]
    query_heads = q_hbm.shape[1] // head_dim
    group = query_heads // kv_heads
    keys = n * part

    barrier = pltpu.get_barrier_semaphore()
    peers = []
    for dz in range(depth):
        for dy in range(2):
            if dz or dy:
                peers.append((lax.rem(z + dz, depth), lax.rem(y + dy, 2)))
    for pz, py in peers:
        pl.semaphore_signal(barrier, inc=1, device_id=device(pz, py, core), device_id_type=MESH)
    pl.semaphore_signal(barrier, inc=1, device_id=device(z, y, 1 - core), device_id_type=MESH)

    def x_block(c, pz, py):
        start = pl.multiple_of((pz * 2 + py) * features, features)
        return x_hbm.at[pl.ds(c * part, part), pl.ds(start, features)]

    own_w = pl.ds(pl.multiple_of(core * w_rows, w_rows), w_rows)
    w_local = pltpu.make_async_copy(w_hbm, w.at[own_w], local_sem.at[0])
    q_local = pltpu.make_async_copy(q_hbm, q_raw, local_sem.at[1])
    x_local = []
    for c in range(chunks):
        x_local.append(pltpu.make_async_copy(x_block(c, z, y), x_in.at[c, y, z], xl_sem.at[c]))
    for d in [w_local, q_local] + x_local:
        d.start()

    pl.semaphore_wait(barrier, len(peers) + 1)

    sent = []

    def send(d):
        d.start()
        sent.append(d)

    w_copy = copy(w_hbm, w.at[own_w], w_send, w_recv, z, y, 1 - core)
    send(w_copy)
    for c in range(chunks):
        for pz, py in peers:
            send(
                copy(
                    x_block(c, pz, py),
                    x_in.at[c, y, z],
                    x_send.at[c, py, pz],
                    x_recv.at[c, y, z],
                    pz,
                    py,
                    core,
                )
            )

    q_local.wait()
    for h in range(query_heads):
        v = q_raw[:, h * head_dim : (h + 1) * head_dim].astype(f32)
        mean = jnp.mean(v * v, axis=-1, keepdims=True)
        v = v * lax.rsqrt(mean + epsilon) * q_gain[...]
        at = (h % group) * text_rows
        q_normed[h // group, at : at + text_rows, :] = v.astype(bf16)

    t_pos = lax.broadcasted_iota(jnp.int32, (text_rows, keys), 0) + me * text_rows
    key = lax.broadcasted_iota(jnp.int32, (text_rows, keys), 1)
    p_first = key // part * rows + key % part
    segment = jnp.zeros((text_rows, keys), jnp.int32)
    t_end = jnp.int32(0)
    for j in range(text_counts.shape[0]):
        t_end = t_end + text_counts[j]
        segment = segment + jnp.where(t_pos >= t_end, 1, 0)
    for c in range(chunks):
        owner = jnp.zeros((text_rows, keys), jnp.int32)
        p_end = jnp.int32(0)
        for j in range(image_counts.shape[0]):
            p_end = p_end + image_counts[j]
            owner = owner + jnp.where(p_first + c * part >= p_end, 1, 0)
        bias[c] = jnp.where(owner <= segment, 0.0, -1e30).astype(f32)

    def project(c):
        x_local[c].wait()
        if c == 0:
            w_local.wait()
            w_copy.wait_recv()
        for pz, py in peers:
            block = x_in.at[c, py, pz]
            copy(
                block, block, x_send.at[c, py, pz], x_recv.at[c, py, pz], pz, py, core
            ).wait_recv()
        block = jnp.concatenate([x_in[c, y], x_in[c, 1 - y]], axis=0)
        block = block.reshape(2 * depth * part, features)
        product = jnp.dot(block, w[...], preferred_element_type=f32)
        product = product.reshape(2, depth, part, kv_cols)
        part_own[c] = product[0]
        part_out[c] = product[1].astype(bf16)
        send(copy(part_out.at[c], y_in.at[c], ry_send.at[c], ry_recv.at[c], z, 1 - y, core))

    def reduce_y(c):
        copy(
            part_out.at[c], y_in.at[c], ry_send.at[c], ry_recv.at[c], z, 1 - y, core
        ).wait_recv()
        for s in range(1, depth):
            zt = lax.rem(z + s, depth)
            z_out[c, zt] = (part_own[c, zt] + y_in[c, zt].astype(f32)).astype(bf16)
            send(
                copy(
                    z_out.at[c, zt],
                    z_in.at[c, z],
                    rz_send.at[c, zt],
                    rz_recv.at[c, z],
                    zt,
                    y,
                    core,
                )
            )

    def reduce_z(c):
        total = part_own[c, z] + y_in[c, z].astype(f32)
        for s in range(1, depth):
            zs = lax.rem(z + depth - s, depth)
            block = z_in.at[c, zs]
            copy(block, block, rz_send.at[c, zs], rz_recv.at[c, zs], zs, y, core).wait_recv()
            total = total + z_in[c, zs].astype(f32)
        for g in range(kv_heads):
            at = slice(g * head_dim, (g + 1) * head_dim)
            v = total[:, at]
            mean = jnp.mean(v * v, axis=-1, keepdims=True)
            kv[c, me, :, at] = (v * lax.rsqrt(mean + epsilon) * k_gain[...]).astype(bf16)
        kv[c, me, :, kv_width:] = total[:, kv_width:].astype(bf16)
        own = kv.at[c, me]
        for s in range(1, depth):
            zt = lax.rem(z + s, depth)
            send(copy(own, own, az_send.at[c, zt], az_recv.at[c, z], zt, y, core))
        send(to_y(c, z))
        send(to_core(c, z, y))

    def to_y(c, zb):
        block = kv.at[c, index(zb, y, core)]
        return copy(block, block, ay_send.at[c, zb], ay_recv.at[c, zb], z, 1 - y, core)

    def to_core(c, zb, yb):
        block = kv.at[c, index(zb, yb, core)]
        return copy(block, block, ac_send.at[c, yb, zb], ac_recv.at[c, yb, zb], z, y, 1 - core)

    def gather_z(c):
        for s in range(1, depth):
            zs = lax.rem(z + depth - s, depth)
            block = kv.at[c, index(zs, y, core)]
            copy(block, block, az_send.at[c, zs], az_recv.at[c, zs], zs, y, core).wait_recv()
            send(to_y(c, zs))
            send(to_core(c, zs, y))

    def gather_y(c):
        for s in range(depth):
            zs = lax.rem(z + depth - s, depth)
            block = kv.at[c, index(zs, 1 - y, core)]
            copy(block, block, ay_send.at[c, zs], ay_recv.at[c, zs], z, 1 - y, core).wait_recv()
            send(to_core(c, zs, 1 - y))

    scale = math.log2(math.e) / math.sqrt(head_dim)
    heads = math.gcd(group, 4)
    tile = heads * text_rows

    def attend(c):
        for zs in range(depth):
            for yb in range(2):
                block = kv.at[c, index(zs, yb, 1 - core)]
                copy(
                    block, block, ac_send.at[c, yb, zs], ac_recv.at[c, yb, zs], z, y, 1 - core
                ).wait_recv()

        @pl.loop(0, kv_heads)
        def _(g):
            k_at = pl.ds(pl.multiple_of(g * head_dim, head_dim), head_dim)
            v_at = pl.ds(pl.multiple_of(kv_width + g * head_dim, head_dim), head_dim)
            key_block = kv[c, :, :, k_at].reshape(keys, head_dim)
            value_block = kv[c, :, :, v_at].reshape(keys, head_dim)
            value_block = jnp.concatenate([value_block, jnp.ones_like(value_block)], axis=1)
            for t in range(group // heads):
                at = slice(t * tile, (t + 1) * tile)
                scores = lax.dot_general(
                    q_normed[g, at, :],
                    key_block,
                    (((1,), (1,)), ((), ())),
                    preferred_element_type=f32,
                )
                scores = scores.reshape(heads, text_rows, keys) * scale + bias[c][None]
                weights = jnp.exp2(scores).astype(bf16).reshape(tile, keys)
                total = jnp.dot(weights, value_block, preferred_element_type=f32)
                if c:
                    total = total + sums[g, at, :]
                if c < chunks - 1:
                    sums[g, at, :] = total
                    continue
                result = (total[:, :head_dim] / total[:, head_dim:]).astype(bf16)
                for i in range(heads):
                    col = pl.multiple_of((g * group + t * heads + i) * head_dim, head_dim)
                    out[:, pl.ds(col, head_dim)] = result[i * text_rows : (i + 1) * text_rows]

    stages = (
        (0.0, project),
        (3.5, reduce_y),
        (7.0, reduce_z),
        (10.0, gather_z),
        (13.0, gather_y),
        (15.6, attend),
    )
    plan = [(6 * c + at, c, i) for c in range(chunks) for i, (at, _) in enumerate(stages)]
    for _, c, i in sorted(plan):
        stages[i][1](c)

    for d in sent:
        d.wait_send()


def body(n, text_queries, image_states, kv_weight, q_gain, k_gain, text_counts, image_counts):
    f32, bf16 = jnp.float32, jnp.bfloat16
    rows = image_states.shape[0]
    features = image_states.shape[1] * 2 // n
    w_rows, kv_cols = kv_weight.shape
    text_rows, q_cols = text_queries.shape
    head_dim = q_gain.shape[0]
    kv_heads = kv_cols // 2 // head_dim
    group = q_cols // head_dim // kv_heads
    depth = n // 4
    part = 16 if rows % 16 == 0 else rows
    chunks = rows // part
    vmem = pl.BlockSpec(memory_space=pltpu.VMEM)
    smem = pl.BlockSpec(memory_space=pltpu.SMEM)
    anywhere = pl.BlockSpec(memory_space=pl.ANY)
    dma = pltpu.SemaphoreType.DMA
    return pl.pallas_call(
        functools.partial(kernel, n),
        out_shape=jax.ShapeDtypeStruct((text_rows, q_cols), bf16),
        in_specs=[anywhere, anywhere, anywhere, vmem, vmem, smem, smem],
        out_specs=vmem,
        scratch_shapes=[
            pltpu.VMEM((text_rows, q_cols), bf16),
            pltpu.VMEM((kv_heads, group * text_rows, head_dim), bf16),
            pltpu.VMEM((chunks, 2, depth, part, features), bf16),
            pltpu.VMEM((2 * w_rows, kv_cols), bf16),
            pltpu.VMEM((chunks, depth, part, kv_cols), f32),
            pltpu.VMEM((chunks, depth, part, kv_cols), bf16),
            pltpu.VMEM((chunks, depth, part, kv_cols), bf16),
            pltpu.VMEM((chunks, depth, part, kv_cols), bf16),
            pltpu.VMEM((chunks, depth, part, kv_cols), bf16),
            pltpu.VMEM((chunks, n, part, kv_cols), bf16),
            pltpu.VMEM((chunks, text_rows, n * part), f32),
            pltpu.VMEM((kv_heads, group * text_rows, 2 * head_dim), f32),
            dma((2,)),
            dma((chunks,)),
            dma((chunks, 2, depth)),
            dma((chunks, 2, depth)),
            dma,
            dma,
            dma((chunks,)),
            dma((chunks,)),
            dma((chunks, depth)),
            dma((chunks, depth)),
            dma((chunks, depth)),
            dma((chunks, depth)),
            dma((chunks, depth)),
            dma((chunks, depth)),
            dma((chunks, 2, depth)),
            dma((chunks, 2, depth)),
        ],
        compiler_params=pltpu.CompilerParams(
            collective_id=0, has_side_effects=True, vmem_limit_bytes=60 << 20
        ),
    )(
        text_queries,
        image_states,
        kv_weight,
        q_gain.reshape(1, head_dim),
        k_gain.reshape(1, head_dim),
        text_counts,
        image_counts,
    )


def solution(mesh):
    placed = (
        P(("groups", "blk"), None),
        P(("groups", "blk"), None),
        P("blk", None),
        P(),
        P(),
        P("groups"),
        P("groups"),
    )
    return jax.shard_map(
        functools.partial(body, mesh.shape["blk"]),
        mesh=mesh,
        in_specs=placed,
        out_specs=P(("groups", "blk"), None),
        check_vma=False,
    )
```

```python
import functools
import math

import jax
import jax.numpy as jnp
from jax import lax
from jax.experimental import pallas as pl
from jax.experimental.pallas import tpu as pltpu
from jax.sharding import PartitionSpec as P

epsilon = 1e-05
MESH = pl.DeviceIdType.MESH


def kernel(
    n,
    q_hbm,
    x_hbm,
    w_hbm,
    q_gain,
    k_gain,
    text_counts,
    image_counts,
    out,
    q_raw,
    q_normed,
    x_in,
    w,
    part,
    y_out,
    y_in,
    z_out,
    z_in,
    kv,
    bias,
    sums,
    local_sem,
    xl_sem,
    x_send,
    x_recv,
    w_send,
    w_recv,
    ry_send,
    ry_recv,
    rz_send,
    rz_recv,
    az_send,
    az_recv,
    ay_send,
    ay_recv,
    ac_send,
    ac_recv,
):
    f32, bf16 = jnp.float32, jnp.bfloat16
    me = lax.axis_index("blk")
    core = lax.rem(me, 2)
    chip = me // 2
    y = lax.rem(chip, 2)
    z = chip // 2
    depth = n // 4
    levels = depth.bit_length() - 1

    def device(z_, y_, core_):
        return {"blk": (z_ * 2 + y_) * 2 + core_}

    def copy(src, dst, send, recv, z_, y_, core_):
        return pltpu.make_async_remote_copy(
            src_ref=src,
            dst_ref=dst,
            send_sem=send,
            recv_sem=recv,
            device_id=device(z_, y_, core_),
            device_id_type=MESH,
        )

    def reverse(v):
        total = 0
        for j in range(levels):
            total = total + v // 2**j % 2 * 2 ** (levels - 1 - j)
        return total

    def flip(v, j):
        return v + 2**j - v // 2**j % 2 * 2 ** (j + 1)

    chunks, _, _, rows_c, features = x_in.shape
    rows, head_dim = x_hbm.shape[0], q_gain.shape[1]
    w_rows, kv_cols = w_hbm.shape
    kv_width = kv_cols // 2
    kv_heads = kv_width // head_dim
    text_rows = q_hbm.shape[0]
    query_heads = q_hbm.shape[1] // head_dim
    group = query_heads // kv_heads
    keys = n * rows_c
    zr = reverse(z)

    barrier = pltpu.get_barrier_semaphore()
    peers = []
    for d in reversed(range(depth)):
        pz = z
        for j in range(levels):
            if d >> j & 1:
                pz = flip(pz, j)
        for py in (y, 1 - y):
            if d or py is not y:
                peers.append((pz, py))
    for pz, py in peers:
        pl.semaphore_signal(barrier, inc=1, device_id=device(pz, py, core), device_id_type=MESH)
    pl.semaphore_signal(barrier, inc=1, device_id=device(z, y, 1 - core), device_id_type=MESH)

    def x_block(c, pz, py):
        start = pl.multiple_of((pz * 2 + py) * features, features)
        return x_hbm.at[pl.ds(c * rows_c, rows_c), pl.ds(start, features)]

    own_w = pl.ds(pl.multiple_of(core * w_rows, w_rows), w_rows)
    w_local = pltpu.make_async_copy(w_hbm, w.at[own_w], local_sem.at[0])
    q_local = pltpu.make_async_copy(q_hbm, q_raw, local_sem.at[1])
    x_local = []
    for c in range(chunks):
        x_local.append(pltpu.make_async_copy(x_block(c, z, y), x_in.at[c, y, zr], xl_sem.at[c]))
    for d in [w_local, q_local] + x_local:
        d.start()

    pl.semaphore_wait(barrier, len(peers) + 1)

    sent = []

    def send(d):
        d.start()
        sent.append(d)

    def send_x(c):
        for pz, py in peers:
            send(
                copy(
                    x_block(c, pz, py),
                    x_in.at[c, y, zr],
                    x_send.at[c, py, pz],
                    x_recv.at[c, y, z],
                    pz,
                    py,
                    core,
                )
            )

    w_copy = copy(w_hbm, w.at[own_w], w_send, w_recv, z, y, 1 - core)
    send_x(0)
    send(w_copy)
    if chunks > 1:
        send_x(1)

    q_local.wait()
    for h in range(query_heads):
        v = q_raw[:, h * head_dim : (h + 1) * head_dim].astype(f32)
        mean = jnp.mean(v * v, axis=-1, keepdims=True)
        v = v * lax.rsqrt(mean + epsilon) * q_gain[...]
        at = (h % group) * text_rows
        q_normed[h // group, at : at + text_rows, :] = v.astype(bf16)

    t_pos = lax.broadcasted_iota(jnp.int32, (text_rows, keys), 0) + me * text_rows
    key = lax.broadcasted_iota(jnp.int32, (1, keys), 1)
    slot = key // rows_c
    key_device = (reverse(slot % depth) * 2 + slot // depth % 2) * 2 + slot // (2 * depth)
    p_first = key_device * rows + key % rows_c
    segment = jnp.zeros((text_rows, keys), jnp.int32)
    t_end = jnp.int32(0)
    for j in range(text_counts.shape[0]):
        t_end = t_end + text_counts[j]
        segment = segment + jnp.where(t_pos >= t_end, 1, 0)
    for c in range(chunks):
        owner = jnp.zeros((1, keys), jnp.int32)
        p_end = jnp.int32(0)
        for j in range(image_counts.shape[0]):
            p_end = p_end + image_counts[j]
            owner = owner + jnp.where(p_first + c * rows_c >= p_end, 1, 0)
        bias[c] = jnp.where(owner <= segment, 0.0, -1e30).astype(f32)

    def project(c):
        x_local[c].wait()
        if c == 0:
            w_local.wait()
            w_copy.wait_recv()
        for pz, py in peers:
            block = x_in.at[c, py, reverse(pz)]
            copy(
                block, block, x_send.at[c, py, pz], x_recv.at[c, py, pz], pz, py, core
            ).wait_recv()
        block = jnp.concatenate([x_in[c, 1 - y], x_in[c, y]], axis=0)
        block = block.reshape(2 * depth * rows_c, features)
        product = jnp.dot(block, w[...], preferred_element_type=f32)
        product = product.reshape(2, depth, rows_c, kv_cols)
        y_out[c] = product[0].astype(bf16)
        send(copy(y_out.at[c], y_in.at[c], ry_send.at[c], ry_recv.at[c], z, 1 - y, core))
        part[c] = product[1]
        if c + 2 < chunks:
            send_x(c + 2)

    def span(count):
        width = depth >> count
        return pl.ds(zr // width * width, width)

    def z_step(c, j):
        width = depth >> (j + 1)
        at = pl.ds(depth - 2 * width, width)
        peer = flip(z, j)
        return copy(
            z_out.at[c, at], z_in.at[c, at], rz_send.at[c, j], rz_recv.at[c, j], peer, y, core
        )

    def send_z(c, j):
        width = depth >> (j + 1)
        base = zr // width * width
        other = base + width - 2 * (zr // width % 2) * width
        z_out[c, depth - 2 * width : depth - width] = part[c, pl.ds(other, width)].astype(bf16)
        send(z_step(c, j))

    def after_sum(c, j):
        if j < levels:
            send_z(c, j)
            return
        total = part[c, zr]
        for g in range(kv_heads):
            at = slice(g * head_dim, (g + 1) * head_dim)
            v = total[:, at]
            mean = jnp.mean(v * v, axis=-1, keepdims=True)
            kv[c, core, y, zr, :, at] = (v * lax.rsqrt(mean + epsilon) * k_gain[...]).astype(bf16)
        kv[c, core, y, zr, :, kv_width:] = total[:, kv_width:].astype(bf16)
        send_gather(c, levels - 1)

    def reduce_y(c):
        copy(y_out.at[c], y_in.at[c], ry_send.at[c], ry_recv.at[c], z, 1 - y, core).wait_recv()
        part[c] += y_in[c].astype(f32)
        after_sum(c, 0)

    def reduce_z(j, c):
        z_step(c, j).wait_recv()
        width = depth >> (j + 1)
        keep = span(j + 1)
        part[c, keep] += z_in[c, depth - 2 * width : depth - width].astype(f32)
        after_sum(c, j + 1)

    def gather_step(c, j):
        if j >= 0:
            block = kv.at[c, core, y, span(j + 1)]
            return copy(
                block, block, az_send.at[c, j], az_recv.at[c, j], flip(z, j), y, core
            )
        if j == -1:
            block = kv.at[c, core, y]
            return copy(block, block, ay_send.at[c], ay_recv.at[c], z, 1 - y, core)
        block = kv.at[c, core]
        return copy(block, block, ac_send.at[c], ac_recv.at[c], z, y, 1 - core)

    def gather_source(c, j):
        if j >= 0:
            width = depth >> (j + 1)
            base = zr // width * width
            other = base + width - 2 * (zr // width % 2) * width
            block = kv.at[c, core, y, pl.ds(other, width)]
            return copy(
                block, block, az_send.at[c, j], az_recv.at[c, j], flip(z, j), y, core
            )
        if j == -1:
            block = kv.at[c, core, 1 - y]
            return copy(block, block, ay_send.at[c], ay_recv.at[c], z, 1 - y, core)
        block = kv.at[c, 1 - core]
        return copy(block, block, ac_send.at[c], ac_recv.at[c], z, y, 1 - core)

    def send_gather(c, j):
        send(gather_step(c, j))

    def gather(j, c):
        gather_source(c, j).wait_recv()
        send_gather(c, j - 1)

    scale = math.log2(math.e) / math.sqrt(head_dim)
    heads = math.gcd(group, 4)
    tile = heads * text_rows

    def attend(g, c):
        if g == 0:
            gather_source(c, -2).wait_recv()
        k_at = slice(g * head_dim, (g + 1) * head_dim)
        v_at = slice(kv_width + g * head_dim, kv_width + (g + 1) * head_dim)
        key_block = kv[c, :, :, :, :, k_at].reshape(keys, head_dim)
        value_block = kv[c, :, :, :, :, v_at].reshape(keys, head_dim)
        value_block = jnp.concatenate([value_block, jnp.ones_like(value_block)], axis=1)
        for t in range(group // heads):
            at = slice(t * tile, (t + 1) * tile)
            scores = lax.dot_general(
                q_normed[g, at, :],
                key_block,
                (((1,), (1,)), ((), ())),
                preferred_element_type=f32,
            )
            scores = scores.reshape(heads, text_rows, keys) * scale + bias[c][None]
            weights = jnp.exp2(scores).astype(bf16).reshape(tile, keys)
            total = jnp.dot(weights, value_block, preferred_element_type=f32)
            if c:
                total = total + sums[g, at, :]
            if c < chunks - 1:
                sums[g, at, :] = total
                continue
            result = (total[:, :head_dim] / total[:, head_dim:]).astype(bf16)
            for i in range(heads):
                col = (g * group + t * heads + i) * head_dim
                out[:, col : col + head_dim] = result[i * text_rows : (i + 1) * text_rows]

    stages = [(0.0, project), (4.0, reduce_y)]
    at = 4.0
    for j in range(levels):
        at += 2.5
        stages.append((at, functools.partial(reduce_z, j)))
    for j in reversed(range(levels)):
        at += 2.5
        stages.append((at, functools.partial(gather, j)))
    stages.append((at + 4.0, functools.partial(gather, -1)))
    for g in range(kv_heads):
        stages.append((at + 5.7 + g, functools.partial(attend, g)))
    plan = [(7 * c + at, c, i) for c in range(chunks) for i, (at, _) in enumerate(stages)]
    for _, c, i in sorted(plan):
        stages[i][1](c)

    for d in sent:
        d.wait_send()


def body(n, text_queries, image_states, kv_weight, q_gain, k_gain, text_counts, image_counts):
    f32, bf16 = jnp.float32, jnp.bfloat16
    rows = image_states.shape[0]
    features = image_states.shape[1] * 2 // n
    w_rows, kv_cols = kv_weight.shape
    text_rows, q_cols = text_queries.shape
    head_dim = q_gain.shape[0]
    kv_heads = kv_cols // 2 // head_dim
    group = q_cols // head_dim // kv_heads
    depth = n // 4
    levels = max(depth.bit_length() - 1, 1)
    rows_c = 16 if rows % 16 == 0 else rows
    chunks = rows // rows_c
    vmem = pl.BlockSpec(memory_space=pltpu.VMEM)
    smem = pl.BlockSpec(memory_space=pltpu.SMEM)
    anywhere = pl.BlockSpec(memory_space=pl.ANY)
    dma = pltpu.SemaphoreType.DMA
    return pl.pallas_call(
        functools.partial(kernel, n),
        out_shape=jax.ShapeDtypeStruct((text_rows, q_cols), bf16),
        in_specs=[anywhere, anywhere, anywhere, vmem, vmem, smem, smem],
        out_specs=vmem,
        scratch_shapes=[
            pltpu.VMEM((text_rows, q_cols), bf16),
            pltpu.VMEM((kv_heads, group * text_rows, head_dim), bf16),
            pltpu.VMEM((chunks, 2, depth, rows_c, features), bf16),
            pltpu.VMEM((2 * w_rows, kv_cols), bf16),
            pltpu.VMEM((chunks, depth, rows_c, kv_cols), f32),
            pltpu.VMEM((chunks, depth, rows_c, kv_cols), bf16),
            pltpu.VMEM((chunks, depth, rows_c, kv_cols), bf16),
            pltpu.VMEM((chunks, depth, rows_c, kv_cols), bf16),
            pltpu.VMEM((chunks, depth, rows_c, kv_cols), bf16),
            pltpu.VMEM((chunks, 2, 2, depth, rows_c, kv_cols), bf16),
            pltpu.VMEM((chunks, text_rows, n * rows_c), f32),
            pltpu.VMEM((kv_heads, group * text_rows, 2 * head_dim), f32),
            dma((2,)),
            dma((chunks,)),
            dma((chunks, 2, depth)),
            dma((chunks, 2, depth)),
            dma,
            dma,
            dma((chunks,)),
            dma((chunks,)),
            dma((chunks, levels)),
            dma((chunks, levels)),
            dma((chunks, levels)),
            dma((chunks, levels)),
            dma((chunks,)),
            dma((chunks,)),
            dma((chunks,)),
            dma((chunks,)),
        ],
        compiler_params=pltpu.CompilerParams(
            collective_id=0, has_side_effects=True, vmem_limit_bytes=60 << 20
        ),
    )(
        text_queries,
        image_states,
        kv_weight,
        q_gain.reshape(1, head_dim),
        k_gain.reshape(1, head_dim),
        text_counts,
        image_counts,
    )


def solution(mesh):
    placed = (
        P(("groups", "blk"), None),
        P(("groups", "blk"), None),
        P("blk", None),
        P(),
        P(),
        P("groups"),
        P("groups"),
    )
    return jax.shard_map(
        functools.partial(body, mesh.shape["blk"]),
        mesh=mesh,
        in_specs=placed,
        out_specs=P(("groups", "blk"), None),
        check_vma=False,
    )
```

```python
import functools
import math

import jax
import jax.numpy as jnp
from jax import lax
from jax.experimental import pallas as pl
from jax.experimental.pallas import tpu as pltpu
from jax.sharding import PartitionSpec as P

epsilon = 1e-05
MESH = pl.DeviceIdType.MESH


def kernel(
    n,
    q_hbm,
    x_hbm,
    w_hbm,
    q_gain,
    k_gain,
    text_counts,
    image_counts,
    out,
    q_raw,
    q_normed,
    x_in,
    w,
    part,
    y_out,
    y_in,
    z_out,
    z_in,
    kv,
    bias,
    local_sem,
    x_send,
    x_recv,
    w_send,
    w_recv,
    ry_send,
    ry_recv,
    rz_send,
    rz_recv,
    az_send,
    az_recv,
    ay_send,
    ay_recv,
    ac_send,
    ac_recv,
):
    f32, bf16 = jnp.float32, jnp.bfloat16
    me = lax.axis_index("blk")
    core = lax.rem(me, 2)
    chip = me // 2
    y = lax.rem(chip, 2)
    z = chip // 2
    depth = n // 4
    levels = depth.bit_length() - 1

    def device(z_, y_, core_):
        return {"blk": (z_ * 2 + y_) * 2 + core_}

    def copy(src, dst, send, recv, z_, y_, core_):
        return pltpu.make_async_remote_copy(
            src_ref=src,
            dst_ref=dst,
            send_sem=send,
            recv_sem=recv,
            device_id=device(z_, y_, core_),
            device_id_type=MESH,
        )

    def other(d):
        v = z
        for j in range(levels):
            if d >> j & 1:
                v = v + 2**j - v // 2**j % 2 * 2 ** (j + 1)
        return v

    zs = [other(d) for d in range(depth)]
    _, _, rows, features = x_in.shape
    head_dim = q_gain.shape[1]
    w_rows, kv_cols = w_hbm.shape
    kv_width = kv_cols // 2
    kv_heads = kv_width // head_dim
    text_rows = q_hbm.shape[0]
    query_heads = q_hbm.shape[1] // head_dim
    group = query_heads // kv_heads
    keys = n * rows
    pieces = kv.shape[0]
    width = kv_width // pieces
    piece_heads = kv_heads // pieces

    far = [(d, py) for d in range(depth // 2, depth) for py in (y, 1 - y)]
    near = [(d, py) for d in reversed(range(depth // 2)) for py in (y, 1 - y)]
    peers = [p for pair in zip(far, near) for p in pair if p[0] or p[1] is not y]
    barrier = pltpu.get_barrier_semaphore()
    for d, py in peers:
        pl.semaphore_signal(
            barrier, inc=1, device_id=device(zs[d], py, core), device_id_type=MESH
        )
    pl.semaphore_signal(barrier, inc=1, device_id=device(z, y, 1 - core), device_id_type=MESH)

    def x_block(pz, py):
        start = pl.multiple_of((pz * 2 + py) * features, features)
        return x_hbm.at[:, pl.ds(start, features)]

    own_w = pl.ds(pl.multiple_of(core * w_rows, w_rows), w_rows)
    x_local = pltpu.make_async_copy(x_block(z, y), x_in.at[y, z], local_sem.at[0])
    w_local = pltpu.make_async_copy(w_hbm, w.at[own_w], local_sem.at[1])
    q_local = pltpu.make_async_copy(q_hbm, q_raw, local_sem.at[2])
    x_local.start()
    w_local.start()
    q_local.start()

    pl.semaphore_wait(barrier, len(peers) + 1)

    sent = []

    def send(d):
        d.start()
        sent.append(d)

    for d, py in peers:
        send(
            copy(
                x_block(zs[d], py),
                x_in.at[y, z],
                x_send.at[py, zs[d]],
                x_recv.at[y, z],
                zs[d],
                py,
                core,
            )
        )
    w_copy = copy(w_hbm, w.at[own_w], w_send, w_recv, z, y, 1 - core)
    send(w_copy)

    q_local.wait()
    for h in range(query_heads):
        v = q_raw[:, h * head_dim : (h + 1) * head_dim].astype(f32)
        mean = jnp.mean(v * v, axis=-1, keepdims=True)
        v = v * lax.rsqrt(mean + epsilon) * q_gain[...]
        at = (h % group) * text_rows
        q_normed[h // group, at : at + text_rows, :] = v.astype(bf16)

    t_pos = lax.broadcasted_iota(jnp.int32, (text_rows, keys), 0) + me * text_rows
    key = lax.broadcasted_iota(jnp.int32, (1, keys), 1)
    slot = key // rows
    key_device = (slot % depth * 2 + slot // depth % 2) * 2 + slot // (2 * depth)
    p_pos = key_device * rows + key % rows
    segment = jnp.zeros((text_rows, keys), jnp.int32)
    owner = jnp.zeros((1, keys), jnp.int32)
    t_end, p_end = jnp.int32(0), jnp.int32(0)
    for j in range(text_counts.shape[0]):
        t_end = t_end + text_counts[j]
        p_end = p_end + image_counts[j]
        segment = segment + jnp.where(t_pos >= t_end, 1, 0)
        owner = owner + jnp.where(p_pos >= p_end, 1, 0)
    bias[...] = jnp.where(owner <= segment, 0.0, -1e30).astype(f32)

    x_local.wait()
    w_local.wait()
    w_copy.wait_recv()

    def project(d):
        at = zs[d]
        for py in (y, 1 - y):
            if d or py is not y:
                block = x_in.at[py, at]
                copy(block, block, x_send.at[py, at], x_recv.at[py, at], at, py, core).wait_recv()
        block = jnp.concatenate([x_in[y, at], x_in[1 - y, at]], axis=0)
        for h in range(pieces):
            for i in range(2):
                cols = slice(i * kv_width + h * width, i * kv_width + (h + 1) * width)
                product = jnp.dot(block, w[:, cols], preferred_element_type=f32)
                cols = slice(i * width, (i + 1) * width)
                part[h, at, :, cols] = product[:rows]
                y_out[h, at, :, cols] = product[rows:].astype(bf16)
            send(y_step(h, at))

    def y_step(h, at):
        return copy(
            y_out.at[h, at], y_in.at[h, at], ry_send.at[h, at], ry_recv.at[h, at], z, 1 - y, core
        )

    def reduce_y(h, d):
        at = zs[d]
        y_step(h, at).wait_recv()
        z_out[h, at] = (part[h, at] + y_in[h, at].astype(f32)).astype(bf16)
        send(
            copy(
                z_out.at[h, at], z_in.at[h, z], rz_send.at[h, at], rz_recv.at[h, z], at, y, core
            )
        )

    def finish(h):
        y_step(h, z).wait_recv()
        total = part[h, z] + y_in[h, z].astype(f32)
        for at in zs[1:]:
            block = z_in.at[h, at]
            copy(block, block, rz_send.at[h, at], rz_recv.at[h, at], at, y, core).wait_recv()
            total = total + z_in[h, at].astype(f32)
        for g in range(piece_heads):
            at = slice(g * head_dim, (g + 1) * head_dim)
            v = total[:, at]
            mean = jnp.mean(v * v, axis=-1, keepdims=True)
            kv[h, core, y, z, :, at] = (v * lax.rsqrt(mean + epsilon) * k_gain[...]).astype(bf16)
        kv[h, core, y, z, :, width:] = total[:, width:].astype(bf16)
        own = kv.at[h, core, y, z]
        for at in reversed(zs[1:]):
            send(copy(own, own, az_send.at[h, at], az_recv.at[h, z], at, y, core))
        send(to_y(h, z))

    def to_y(h, at):
        block = kv.at[h, core, y, at]
        return copy(block, block, ay_send.at[h, at], ay_recv.at[h, at], z, 1 - y, core)

    def column(h, core_, y_):
        block = kv.at[h, core_, y_]
        return copy(block, block, ac_send.at[h, y_], ac_recv.at[h, y_], z, y, 1 - core)

    def gather_z(h):
        for at in zs[1:]:
            block = kv.at[h, core, y, at]
            copy(block, block, az_send.at[h, at], az_recv.at[h, at], at, y, core).wait_recv()
            send(to_y(h, at))
        send(column(h, core, y))

    def gather_y(h):
        for at in zs:
            block = kv.at[h, core, 1 - y, at]
            copy(block, block, ay_send.at[h, at], ay_recv.at[h, at], z, 1 - y, core).wait_recv()
        send(column(h, core, 1 - y))

    scale = math.log2(math.e) / math.sqrt(head_dim)
    pair = math.gcd(group, 2)
    tile = pair * text_rows

    def attend(h, i):
        if i == 0:
            for yb in (y, 1 - y):
                column(h, 1 - core, yb).wait_recv()
        g = h * piece_heads + i
        k_at = slice(i * head_dim, (i + 1) * head_dim)
        v_at = slice(width + i * head_dim, width + (i + 1) * head_dim)
        key_block = kv[h, :, :, :, :, k_at].reshape(keys, head_dim)
        value_block = kv[h, :, :, :, :, v_at].reshape(keys, head_dim)
        value_block = jnp.concatenate([value_block, jnp.ones_like(value_block)], axis=1)
        for t in range(group // pair):
            scores = lax.dot_general(
                q_normed[g, t * tile : (t + 1) * tile, :],
                key_block,
                (((1,), (1,)), ((), ())),
                preferred_element_type=f32,
            )
            scores = scores.reshape(pair, text_rows, keys) * scale + bias[...][None]
            weights = jnp.exp2(scores).astype(bf16).reshape(tile, keys)
            total = jnp.dot(weights, value_block, preferred_element_type=f32)
            result = (total[:, :head_dim] / total[:, head_dim:]).astype(bf16)
            for a in range(pair):
                col = (g * group + t * pair + a) * head_dim
                out[:, col : col + head_dim] = result[a * text_rows : (a + 1) * text_rows]

    for d in range(depth):
        project(d)
        if d > 1:
            for h in range(pieces):
                reduce_y(h, d - 1)
    if depth > 1:
        for h in range(pieces):
            reduce_y(h, depth - 1)
    for h in range(pieces):
        finish(h)
    waiting = []
    for h in range(pieces):
        gather_z(h)
        if waiting:
            attend(*waiting.pop(0))
        gather_y(h)
        for p in waiting:
            attend(*p)
        waiting = [(h, i) for i in range(piece_heads)]
    for p in waiting:
        attend(*p)

    for d in sent:
        d.wait_send()


def body(n, text_queries, image_states, kv_weight, q_gain, k_gain, text_counts, image_counts):
    f32, bf16 = jnp.float32, jnp.bfloat16
    rows = image_states.shape[0]
    features = image_states.shape[1] * 2 // n
    w_rows, kv_cols = kv_weight.shape
    text_rows, q_cols = text_queries.shape
    head_dim = q_gain.shape[0]
    kv_heads = kv_cols // 2 // head_dim
    group = q_cols // head_dim // kv_heads
    depth = n // 4
    pieces = math.gcd(kv_heads, 2)
    cols = kv_cols // pieces
    vmem = pl.BlockSpec(memory_space=pltpu.VMEM)
    smem = pl.BlockSpec(memory_space=pltpu.SMEM)
    anywhere = pl.BlockSpec(memory_space=pl.ANY)
    dma = pltpu.SemaphoreType.DMA
    return pl.pallas_call(
        functools.partial(kernel, n),
        out_shape=jax.ShapeDtypeStruct((text_rows, q_cols), bf16),
        in_specs=[anywhere, anywhere, anywhere, vmem, vmem, smem, smem],
        out_specs=vmem,
        scratch_shapes=[
            pltpu.VMEM((text_rows, q_cols), bf16),
            pltpu.VMEM((kv_heads, group * text_rows, head_dim), bf16),
            pltpu.VMEM((2, depth, rows, features), bf16),
            pltpu.VMEM((2 * w_rows, kv_cols), bf16),
            pltpu.VMEM((pieces, depth, rows, cols), f32),
            pltpu.VMEM((pieces, depth, rows, cols), bf16),
            pltpu.VMEM((pieces, depth, rows, cols), bf16),
            pltpu.VMEM((pieces, depth, rows, cols), bf16),
            pltpu.VMEM((pieces, depth, rows, cols), bf16),
            pltpu.VMEM((pieces, 2, 2, depth, rows, cols), bf16),
            pltpu.VMEM((text_rows, n * rows), f32),
            dma((3,)),
            dma((2, depth)),
            dma((2, depth)),
            dma,
            dma,
            dma((pieces, depth)),
            dma((pieces, depth)),
            dma((pieces, depth)),
            dma((pieces, depth)),
            dma((pieces, depth)),
            dma((pieces, depth)),
            dma((pieces, depth)),
            dma((pieces, depth)),
            dma((pieces, 2)),
            dma((pieces, 2)),
        ],
        compiler_params=pltpu.CompilerParams(
            collective_id=0, has_side_effects=True, vmem_limit_bytes=60 << 20
        ),
    )(
        text_queries,
        image_states,
        kv_weight,
        q_gain.reshape(1, head_dim),
        k_gain.reshape(1, head_dim),
        text_counts,
        image_counts,
    )


def solution(mesh):
    placed = (
        P(("groups", "blk"), None),
        P(("groups", "blk"), None),
        P("blk", None),
        P(),
        P(),
        P("groups"),
        P("groups"),
    )
    return jax.shard_map(
        functools.partial(body, mesh.shape["blk"]),
        mesh=mesh,
        in_specs=placed,
        out_specs=P(("groups", "blk"), None),
        check_vma=False,
    )
```

```python
import functools
import math

import jax
import jax.numpy as jnp
from jax import lax
from jax.experimental import pallas as pl
from jax.experimental.pallas import tpu as pltpu
from jax.sharding import PartitionSpec as P

epsilon = 1e-05
MESH = pl.DeviceIdType.MESH


def kernel(
    n,
    q_hbm,
    x_hbm,
    w_hbm,
    q_gain,
    k_gain,
    text_counts,
    image_counts,
    out,
    q_raw,
    q_normed,
    x_in,
    w,
    part,
    y_out,
    y_in,
    z_out,
    z_in,
    kv,
    bias,
    local_sem,
    x_send,
    x_recv,
    w_send,
    w_recv,
    ry_send,
    ry_recv,
    rz_send,
    rz_recv,
    az_send,
    az_recv,
    ay_send,
    ay_recv,
    ac_send,
    ac_recv,
):
    f32, bf16 = jnp.float32, jnp.bfloat16
    me = lax.axis_index("blk")
    core = lax.rem(me, 2)
    chip = me // 2
    y = lax.rem(chip, 2)
    z = chip // 2
    depth = n // 4
    levels = depth.bit_length() - 1

    def device(z_, y_, core_):
        return {"blk": (z_ * 2 + y_) * 2 + core_}

    def copy(src, dst, send, recv, z_, y_, core_):
        return pltpu.make_async_remote_copy(
            src_ref=src,
            dst_ref=dst,
            send_sem=send,
            recv_sem=recv,
            device_id=device(z_, y_, core_),
            device_id_type=MESH,
        )

    def other(d):
        v = z
        for j in range(levels):
            if d >> j & 1:
                v = v + 2**j - v // 2**j % 2 * 2 ** (j + 1)
        return v

    zs = [other(d) for d in range(depth)]
    _, _, rows, features = x_in.shape
    head_dim = q_gain.shape[1]
    w_rows, kv_cols = w_hbm.shape
    kv_width = kv_cols // 2
    kv_heads = kv_width // head_dim
    text_rows = q_hbm.shape[0]
    query_heads = q_hbm.shape[1] // head_dim
    group = query_heads // kv_heads
    keys = n * rows
    pieces = kv.shape[0]
    width = kv_width // pieces
    piece_heads = kv_heads // pieces

    far = [(d, py) for d in range(depth // 2, depth) for py in (y, 1 - y)]
    near = [(d, py) for d in reversed(range(depth // 2)) for py in (y, 1 - y)]
    peers = [p for pair in zip(far, near) for p in pair if p[0] or p[1] is not y]
    barrier = pltpu.get_barrier_semaphore()
    for d, py in peers:
        pl.semaphore_signal(
            barrier, inc=1, device_id=device(zs[d], py, core), device_id_type=MESH
        )
    pl.semaphore_signal(barrier, inc=1, device_id=device(z, y, 1 - core), device_id_type=MESH)

    def x_block(pz, py):
        start = pl.multiple_of((pz * 2 + py) * features, features)
        return x_hbm.at[:, pl.ds(start, features)]

    own_w = pl.ds(pl.multiple_of(core * w_rows, w_rows), w_rows)
    x_local = pltpu.make_async_copy(x_block(z, y), x_in.at[y, z], local_sem.at[0])
    w_local = pltpu.make_async_copy(w_hbm, w.at[own_w], local_sem.at[1])
    q_local = pltpu.make_async_copy(q_hbm, q_raw, local_sem.at[2])
    x_local.start()
    w_local.start()
    q_local.start()

    pl.semaphore_wait(barrier, len(peers) + 1)

    sent = []

    def send(d):
        d.start()
        sent.append(d)

    w_copy = copy(w_hbm, w.at[own_w], w_send, w_recv, z, y, 1 - core)
    send(w_copy)
    for d, py in peers:
        send(
            copy(
                x_block(zs[d], py),
                x_in.at[y, z],
                x_send.at[py, zs[d]],
                x_recv.at[y, z],
                zs[d],
                py,
                core,
            )
        )

    q_local.wait()
    for h in range(query_heads):
        v = q_raw[:, h * head_dim : (h + 1) * head_dim].astype(f32)
        mean = jnp.mean(v * v, axis=-1, keepdims=True)
        v = v * lax.rsqrt(mean + epsilon) * q_gain[...]
        at = (h % group) * text_rows
        q_normed[h // group, at : at + text_rows, :] = v.astype(bf16)

    t_pos = lax.broadcasted_iota(jnp.int32, (text_rows, keys), 0) + me * text_rows
    key = lax.broadcasted_iota(jnp.int32, (1, keys), 1)
    slot = key // rows
    key_device = (slot % depth * 2 + slot // depth % 2) * 2 + slot // (2 * depth)
    p_pos = key_device * rows + key % rows
    segment = jnp.zeros((text_rows, keys), jnp.int32)
    owner = jnp.zeros((1, keys), jnp.int32)
    t_end, p_end = jnp.int32(0), jnp.int32(0)
    for j in range(text_counts.shape[0]):
        t_end = t_end + text_counts[j]
        p_end = p_end + image_counts[j]
        segment = segment + jnp.where(t_pos >= t_end, 1, 0)
        owner = owner + jnp.where(p_pos >= p_end, 1, 0)
    bias[...] = jnp.where(owner <= segment, 0.0, -1e30).astype(f32)

    x_local.wait()
    w_local.wait()
    w_copy.wait_recv()

    def project(d):
        at = zs[d]
        for py in (y, 1 - y):
            if d or py is not y:
                block = x_in.at[py, at]
                copy(block, block, x_send.at[py, at], x_recv.at[py, at], at, py, core).wait_recv()
        block = jnp.concatenate([x_in[y, at], x_in[1 - y, at]], axis=0)
        for h in range(pieces):
            for i in range(2):
                cols = slice(i * kv_width + h * width, i * kv_width + (h + 1) * width)
                product = jnp.dot(block, w[:, cols], preferred_element_type=f32)
                cols = slice(i * width, (i + 1) * width)
                part[h, at, :, cols] = product[:rows]
                y_out[h, at, :, cols] = product[rows:].astype(bf16)
            send(y_step(h, at))

    def y_step(h, at):
        return copy(
            y_out.at[h, at], y_in.at[h, at], ry_send.at[h, at], ry_recv.at[h, at], z, 1 - y, core
        )

    def reduce_y(h, d):
        at = zs[d]
        y_step(h, at).wait_recv()
        z_out[h, at] = (part[h, at] + y_in[h, at].astype(f32)).astype(bf16)
        send(
            copy(
                z_out.at[h, at], z_in.at[h, z], rz_send.at[h, at], rz_recv.at[h, z], at, y, core
            )
        )

    def finish(h):
        y_step(h, z).wait_recv()
        total = part[h, z] + y_in[h, z].astype(f32)
        for at in zs[1:]:
            block = z_in.at[h, at]
            copy(block, block, rz_send.at[h, at], rz_recv.at[h, at], at, y, core).wait_recv()
            total = total + z_in[h, at].astype(f32)
        for g in range(piece_heads):
            at = slice(g * head_dim, (g + 1) * head_dim)
            v = total[:, at]
            mean = jnp.mean(v * v, axis=-1, keepdims=True)
            kv[h, core, y, z, :, at] = (v * lax.rsqrt(mean + epsilon) * k_gain[...]).astype(bf16)
        kv[h, core, y, z, :, width:] = total[:, width:].astype(bf16)
        own = kv.at[h, core, y, z]
        for j in reversed(range(levels)):
            send(to_z(h, 0, j))
        send(to_y(h, z))

    def to_z(h, d, j):
        block = kv.at[h, core, y, zs[d]]
        return copy(
            block, block, az_send.at[h, zs[d], j], az_recv.at[h, zs[d]], zs[1 << j], y, core
        )

    def to_y(h, at):
        block = kv.at[h, core, y, at]
        return copy(block, block, ay_send.at[h, at], ay_recv.at[h, at], z, 1 - y, core)

    def column(h, core_, y_):
        block = kv.at[h, core_, y_]
        return copy(block, block, ac_send.at[h, y_], ac_recv.at[h, y_], z, y, 1 - core)

    def gather_z(h):
        for d in sorted(range(1, depth), key=lambda d: -(d & -d)):
            lowest = (d & -d).bit_length() - 1
            to_z(h, d, lowest).wait_recv()
            for j in reversed(range(lowest)):
                send(to_z(h, d, j))
            send(to_y(h, zs[d]))
        send(column(h, core, y))

    def gather_y(h):
        for at in zs:
            block = kv.at[h, core, 1 - y, at]
            copy(block, block, ay_send.at[h, at], ay_recv.at[h, at], z, 1 - y, core).wait_recv()
        send(column(h, core, 1 - y))

    scale = math.log2(math.e) / math.sqrt(head_dim)
    pair = math.gcd(group, 2)
    tile = pair * text_rows

    def attend(h, i):
        if i == 0:
            for yb in (y, 1 - y):
                column(h, 1 - core, yb).wait_recv()
        g = h * piece_heads + i
        k_at = slice(i * head_dim, (i + 1) * head_dim)
        v_at = slice(width + i * head_dim, width + (i + 1) * head_dim)
        key_block = kv[h, :, :, :, :, k_at].reshape(keys, head_dim)
        value_block = kv[h, :, :, :, :, v_at].reshape(keys, head_dim)
        value_block = jnp.concatenate([value_block, jnp.ones_like(value_block)], axis=1)
        for t in range(group // pair):
            scores = lax.dot_general(
                q_normed[g, t * tile : (t + 1) * tile, :],
                key_block,
                (((1,), (1,)), ((), ())),
                preferred_element_type=f32,
            )
            scores = scores.reshape(pair, text_rows, keys) * scale + bias[...][None]
            weights = jnp.exp2(scores).astype(bf16).reshape(tile, keys)
            total = jnp.dot(weights, value_block, preferred_element_type=f32)
            result = (total[:, :head_dim] / total[:, head_dim:]).astype(bf16)
            for a in range(pair):
                col = (g * group + t * pair + a) * head_dim
                out[:, col : col + head_dim] = result[a * text_rows : (a + 1) * text_rows]

    for d in range(depth):
        project(d)
        if d > 1:
            for h in range(pieces):
                reduce_y(h, d - 1)
    if depth > 1:
        for h in range(pieces):
            reduce_y(h, depth - 1)
    for h in range(pieces):
        finish(h)
    waiting = []
    for h in range(pieces):
        gather_z(h)
        if waiting:
            attend(*waiting.pop(0))
        gather_y(h)
        for p in waiting:
            attend(*p)
        waiting = [(h, i) for i in range(piece_heads)]
    for p in waiting:
        attend(*p)

    for d in sent:
        d.wait_send()


def body(n, text_queries, image_states, kv_weight, q_gain, k_gain, text_counts, image_counts):
    f32, bf16 = jnp.float32, jnp.bfloat16
    rows = image_states.shape[0]
    features = image_states.shape[1] * 2 // n
    w_rows, kv_cols = kv_weight.shape
    text_rows, q_cols = text_queries.shape
    head_dim = q_gain.shape[0]
    kv_heads = kv_cols // 2 // head_dim
    group = q_cols // head_dim // kv_heads
    depth = n // 4
    pieces = math.gcd(kv_heads, 2)
    cols = kv_cols // pieces
    vmem = pl.BlockSpec(memory_space=pltpu.VMEM)
    smem = pl.BlockSpec(memory_space=pltpu.SMEM)
    anywhere = pl.BlockSpec(memory_space=pl.ANY)
    dma = pltpu.SemaphoreType.DMA
    return pl.pallas_call(
        functools.partial(kernel, n),
        out_shape=jax.ShapeDtypeStruct((text_rows, q_cols), bf16),
        in_specs=[anywhere, anywhere, anywhere, vmem, vmem, smem, smem],
        out_specs=vmem,
        scratch_shapes=[
            pltpu.VMEM((text_rows, q_cols), bf16),
            pltpu.VMEM((kv_heads, group * text_rows, head_dim), bf16),
            pltpu.VMEM((2, depth, rows, features), bf16),
            pltpu.VMEM((2 * w_rows, kv_cols), bf16),
            pltpu.VMEM((pieces, depth, rows, cols), f32),
            pltpu.VMEM((pieces, depth, rows, cols), bf16),
            pltpu.VMEM((pieces, depth, rows, cols), bf16),
            pltpu.VMEM((pieces, depth, rows, cols), bf16),
            pltpu.VMEM((pieces, depth, rows, cols), bf16),
            pltpu.VMEM((pieces, 2, 2, depth, rows, cols), bf16),
            pltpu.VMEM((text_rows, n * rows), f32),
            dma((3,)),
            dma((2, depth)),
            dma((2, depth)),
            dma,
            dma,
            dma((pieces, depth)),
            dma((pieces, depth)),
            dma((pieces, depth)),
            dma((pieces, depth)),
            dma((pieces, depth, max(depth.bit_length() - 1, 1))),
            dma((pieces, depth)),
            dma((pieces, depth)),
            dma((pieces, depth)),
            dma((pieces, 2)),
            dma((pieces, 2)),
        ],
        compiler_params=pltpu.CompilerParams(
            collective_id=0, has_side_effects=True, vmem_limit_bytes=60 << 20
        ),
    )(
        text_queries,
        image_states,
        kv_weight,
        q_gain.reshape(1, head_dim),
        k_gain.reshape(1, head_dim),
        text_counts,
        image_counts,
    )


def solution(mesh):
    placed = (
        P(("groups", "blk"), None),
        P(("groups", "blk"), None),
        P("blk", None),
        P(),
        P(),
        P("groups"),
        P("groups"),
    )
    return jax.shard_map(
        functools.partial(body, mesh.shape["blk"]),
        mesh=mesh,
        in_specs=placed,
        out_specs=P(("groups", "blk"), None),
        check_vma=False,
    )
```

```python
import functools
import math

import jax
import jax.numpy as jnp
from jax import lax
from jax.experimental import pallas as pl
from jax.experimental.pallas import tpu as pltpu
from jax.sharding import PartitionSpec as P

epsilon = 1e-05
MESH = pl.DeviceIdType.MESH


def kernel(
    n,
    groups,
    q_hbm,
    x_hbm,
    w_hbm,
    q_gain,
    k_gain,
    text_counts,
    image_counts,
    out,
    q_raw,
    q_normed,
    x_in,
    w,
    part,
    z_out,
    z_in,
    kv,
    bias,
    local_sem,
    x_send,
    x_recv,
    wc_send,
    wc_recv,
    wy_send,
    wy_recv,
    wx_send,
    wx_recv,
    rz_send,
    rz_recv,
    az_send,
    az_recv,
    ay_send,
    ay_recv,
    ac_send,
    ac_recv,
):
    f32, bf16 = jnp.float32, jnp.bfloat16
    me = lax.axis_index("blk")
    core = lax.rem(me, 2)
    chip = me // 2
    y = lax.rem(chip, 2)
    z = chip // 2
    part_index = lax.axis_index("groups")
    shares = 2 if groups % 2 == 0 else 1
    share = lax.rem(part_index, shares)
    depth = n // 4
    levels = depth.bit_length() - 1

    def device(z_, y_, core_):
        return {"blk": (z_ * 2 + y_) * 2 + core_}

    def copy(src, dst, send, recv, z_, y_, core_):
        return pltpu.make_async_remote_copy(
            src_ref=src,
            dst_ref=dst,
            send_sem=send,
            recv_sem=recv,
            device_id=device(z_, y_, core_),
            device_id_type=MESH,
        )

    def other(d):
        v = z
        for j in range(levels):
            if d >> j & 1:
                v = v + 2**j - v // 2**j % 2 * 2 ** (j + 1)
        return v

    zs = [other(d) for d in range(depth)]
    _, rows, features = x_in.shape
    head_dim = q_gain.shape[1]
    w_rows, kv_cols = w_hbm.shape
    kv_width = kv_cols // 2
    kv_heads = kv_width // head_dim
    text_rows = q_hbm.shape[0]
    query_heads = q_hbm.shape[1] // head_dim
    group = query_heads // kv_heads
    keys = n * rows
    pieces = kv.shape[0]
    width = kv_width // pieces
    piece_heads = kv_heads // pieces

    peers = [device(at, y, core) for at in zs[1:]]
    peers += [device(z, 1 - y, core), device(z, y, 1 - core)]
    if shares == 2:
        peers.append({"groups": part_index + 1 - 2 * share, "blk": me})
    barrier = pltpu.get_barrier_semaphore()
    for peer in peers:
        pl.semaphore_signal(barrier, inc=1, device_id=peer, device_id_type=MESH)

    def x_block(pz):
        return x_hbm.at[:, pl.ds(pl.multiple_of(pz * features, features), features)]

    def w_block(y_, core_, share_):
        size = w_rows // shares
        start = (y_ * 2 + core_) * w_rows + share_ * size
        return w.at[pl.ds(pl.multiple_of(start, size), size)]

    own_w = w.at[pl.ds(pl.multiple_of((y * 2 + core) * w_rows, w_rows), w_rows)]
    x_local = pltpu.make_async_copy(x_block(z), x_in.at[z], local_sem.at[0])
    w_local = pltpu.make_async_copy(w_hbm, own_w, local_sem.at[1])
    q_local = pltpu.make_async_copy(q_hbm, q_raw, local_sem.at[2])
    x_local.start()
    w_local.start()
    q_local.start()

    pl.semaphore_wait(barrier, len(peers))

    sent = []

    def send(d):
        d.start()
        sent.append(d)

    size = w_rows // shares
    w_share = w_hbm.at[pl.ds(pl.multiple_of(share * size, size), size)]
    w_y = copy(w_share, w_block(y, core, share), wy_send, wy_recv, z, 1 - y, core)
    w_c = copy(w_hbm, own_w, wc_send.at[0], wc_recv.at[0], z, y, 1 - core)

    def w_forward(share_, i):
        block = w_block(1 - y, core, share_)
        return copy(block, block, wc_send.at[i], wc_recv.at[i], z, y, 1 - core)

    def x_step(at):
        return copy(x_block(at), x_in.at[z], x_send.at[at], x_recv.at[z], at, y, core)

    send(w_y)
    for at in reversed(zs[1:]):
        send(x_step(at))
    send(w_c)

    q_local.wait()
    for h in range(query_heads):
        v = q_raw[:, h * head_dim : (h + 1) * head_dim].astype(f32)
        mean = jnp.mean(v * v, axis=-1, keepdims=True)
        v = v * lax.rsqrt(mean + epsilon) * q_gain[...]
        at = (h % group) * text_rows
        q_normed[h // group, at : at + text_rows, :] = v.astype(bf16)

    t_pos = lax.broadcasted_iota(jnp.int32, (text_rows, keys), 0) + me * text_rows
    key = lax.broadcasted_iota(jnp.int32, (1, keys), 1)
    slot = key // rows
    key_device = (slot % depth * 2 + slot // depth % 2) * 2 + slot // (2 * depth)
    p_pos = key_device * rows + key % rows
    segment = jnp.zeros((text_rows, keys), jnp.int32)
    owner = jnp.zeros((1, keys), jnp.int32)
    t_end, p_end = jnp.int32(0), jnp.int32(0)
    for j in range(text_counts.shape[0]):
        t_end = t_end + text_counts[j]
        p_end = p_end + image_counts[j]
        segment = segment + jnp.where(t_pos >= t_end, 1, 0)
        owner = owner + jnp.where(p_pos >= p_end, 1, 0)
    bias[...] = jnp.where(owner <= segment, 0.0, -1e30).astype(f32)

    w_y.wait_recv()
    if shares == 2:
        block = w_block(1 - y, core, share)
        w_x = pltpu.make_async_remote_copy(
            src_ref=block,
            dst_ref=block,
            send_sem=wx_send,
            recv_sem=wx_recv,
            device_id=peers[-1],
            device_id_type=MESH,
        )
        send(w_x)
    send(w_forward(share, 1))
    if shares == 2:
        w_x.wait_recv()
        send(w_forward(1 - share, 2))
    x_local.wait()
    w_local.wait()
    w_c.wait_recv()
    w_forward(share, 1).wait_recv()
    if shares == 2:
        w_forward(1 - share, 2).wait_recv()

    def z_step(h, at):
        return copy(
            z_out.at[h, at], z_in.at[h, z], rz_send.at[h, at], rz_recv.at[h, z], at, y, core
        )

    def project(slices):
        for at in slices:
            if at is not z:
                block = x_in.at[at]
                copy(block, block, x_send.at[at], x_recv.at[at], at, y, core).wait_recv()
        block = jnp.concatenate([x_in[at] for at in slices], axis=0)
        for h in range(pieces):
            for i in range(2):
                cols = slice(i * kv_width + h * width, i * kv_width + (h + 1) * width)
                product = jnp.dot(block, w[:, cols], preferred_element_type=f32)
                cols = slice(i * width, (i + 1) * width)
                for a, at in enumerate(slices):
                    piece = product[a * rows : (a + 1) * rows]
                    if at is z:
                        part[h, :, cols] = piece
                    else:
                        z_out[h, at, :, cols] = piece.astype(bf16)
            for at in slices:
                if at is not z:
                    send(z_step(h, at))

    def finish(h):
        total = part[h]
        for at in zs[1:]:
            block = z_in.at[h, at]
            copy(block, block, rz_send.at[h, at], rz_recv.at[h, at], at, y, core).wait_recv()
            total = total + z_in[h, at].astype(f32)
        for g in range(piece_heads):
            at = slice(g * head_dim, (g + 1) * head_dim)
            v = total[:, at]
            mean = jnp.mean(v * v, axis=-1, keepdims=True)
            kv[h, core, y, z, :, at] = (v * lax.rsqrt(mean + epsilon) * k_gain[...]).astype(bf16)
        kv[h, core, y, z, :, width:] = total[:, width:].astype(bf16)
        own = kv.at[h, core, y, z]
        for at in reversed(zs[1:]):
            send(copy(own, own, az_send.at[h, at], az_recv.at[h, z], at, y, core))
        send(to_y(h, z))

    def to_y(h, at):
        block = kv.at[h, core, y, at]
        return copy(block, block, ay_send.at[h, at], ay_recv.at[h, at], z, 1 - y, core)

    def column(h, core_, y_):
        block = kv.at[h, core_, y_]
        return copy(block, block, ac_send.at[h, y_], ac_recv.at[h, y_], z, y, 1 - core)

    def gather_z(h):
        for at in zs[1:]:
            block = kv.at[h, core, y, at]
            copy(block, block, az_send.at[h, at], az_recv.at[h, at], at, y, core).wait_recv()
            send(to_y(h, at))
        send(column(h, core, y))

    def gather_y(h):
        for at in zs:
            block = kv.at[h, core, 1 - y, at]
            copy(block, block, ay_send.at[h, at], ay_recv.at[h, at], z, 1 - y, core).wait_recv()
        send(column(h, core, 1 - y))

    scale = math.log2(math.e) / math.sqrt(head_dim)
    pair = math.gcd(group, 2)
    tile = pair * text_rows

    def attend(h, i):
        if i == 0:
            for yb in (y, 1 - y):
                column(h, 1 - core, yb).wait_recv()
        g = h * piece_heads + i
        k_at = slice(i * head_dim, (i + 1) * head_dim)
        v_at = slice(width + i * head_dim, width + (i + 1) * head_dim)
        key_block = kv[h, :, :, :, :, k_at].reshape(keys, head_dim)
        value_block = kv[h, :, :, :, :, v_at].reshape(keys, head_dim)
        value_block = jnp.concatenate([value_block, jnp.ones_like(value_block)], axis=1)
        for t in range(group // pair):
            scores = lax.dot_general(
                q_normed[g, t * tile : (t + 1) * tile, :],
                key_block,
                (((1,), (1,)), ((), ())),
                preferred_element_type=f32,
            )
            scores = scores.reshape(pair, text_rows, keys) * scale + bias[...][None]
            weights = jnp.exp2(scores).astype(bf16).reshape(tile, keys)
            total = jnp.dot(weights, value_block, preferred_element_type=f32)
            result = (total[:, :head_dim] / total[:, head_dim:]).astype(bf16)
            for a in range(pair):
                col = (g * group + t * pair + a) * head_dim
                out[:, col : col + head_dim] = result[a * text_rows : (a + 1) * text_rows]

    for d in range(0, depth, 2):
        project(zs[d : d + 2])
    for h in range(pieces):
        finish(h)
    waiting = []
    for h in range(pieces):
        gather_z(h)
        if waiting:
            attend(*waiting.pop(0))
        gather_y(h)
        for p in waiting:
            attend(*p)
        waiting = [(h, i) for i in range(piece_heads)]
    for p in waiting:
        attend(*p)

    for d in sent:
        d.wait_send()


def body(n, groups, text_queries, image_states, kv_weight, q_gain, k_gain, text_counts, image_counts):
    f32, bf16 = jnp.float32, jnp.bfloat16
    rows = image_states.shape[0]
    features = image_states.shape[1] * 4 // n
    w_rows, kv_cols = kv_weight.shape
    text_rows, q_cols = text_queries.shape
    head_dim = q_gain.shape[0]
    kv_heads = kv_cols // 2 // head_dim
    group = q_cols // head_dim // kv_heads
    depth = n // 4
    pieces = math.gcd(kv_heads, 2)
    cols = kv_cols // pieces
    vmem = pl.BlockSpec(memory_space=pltpu.VMEM)
    smem = pl.BlockSpec(memory_space=pltpu.SMEM)
    anywhere = pl.BlockSpec(memory_space=pl.ANY)
    dma = pltpu.SemaphoreType.DMA
    return pl.pallas_call(
        functools.partial(kernel, n, groups),
        out_shape=jax.ShapeDtypeStruct((text_rows, q_cols), bf16),
        in_specs=[anywhere, anywhere, anywhere, vmem, vmem, smem, smem],
        out_specs=vmem,
        scratch_shapes=[
            pltpu.VMEM((text_rows, q_cols), bf16),
            pltpu.VMEM((kv_heads, group * text_rows, head_dim), bf16),
            pltpu.VMEM((depth, rows, features), bf16),
            pltpu.VMEM((4 * w_rows, kv_cols), bf16),
            pltpu.VMEM((pieces, rows, cols), f32),
            pltpu.VMEM((pieces, depth, rows, cols), bf16),
            pltpu.VMEM((pieces, depth, rows, cols), bf16),
            pltpu.VMEM((pieces, 2, 2, depth, rows, cols), bf16),
            pltpu.VMEM((text_rows, n * rows), f32),
            dma((3,)),
            dma((depth,)),
            dma((depth,)),
            dma((3,)),
            dma((3,)),
            dma,
            dma,
            dma,
            dma,
            dma((pieces, depth)),
            dma((pieces, depth)),
            dma((pieces, depth)),
            dma((pieces, depth)),
            dma((pieces, depth)),
            dma((pieces, depth)),
            dma((pieces, 2)),
            dma((pieces, 2)),
        ],
        compiler_params=pltpu.CompilerParams(
            collective_id=0, has_side_effects=True, vmem_limit_bytes=60 << 20
        ),
    )(
        text_queries,
        image_states,
        kv_weight,
        q_gain.reshape(1, head_dim),
        k_gain.reshape(1, head_dim),
        text_counts,
        image_counts,
    )


def solution(mesh):
    placed = (
        P(("groups", "blk"), None),
        P(("groups", "blk"), None),
        P("blk", None),
        P(),
        P(),
        P("groups"),
        P("groups"),
    )
    return jax.shard_map(
        functools.partial(body, mesh.shape["blk"], mesh.shape["groups"]),
        mesh=mesh,
        in_specs=placed,
        out_specs=P(("groups", "blk"), None),
        check_vma=False,
    )
```

```python
import functools
import math

import jax
import jax.numpy as jnp
from jax import lax
from jax.experimental import pallas as pl
from jax.experimental.pallas import tpu as pltpu
from jax.sharding import PartitionSpec as P

epsilon = 1e-05
MESH = pl.DeviceIdType.MESH


def kernel(
    n,
    groups,
    q_hbm,
    x_hbm,
    w_hbm,
    q_gain,
    k_gain,
    text_counts,
    image_counts,
    out,
    q_raw,
    q_normed,
    x_in,
    w,
    part,
    z_out,
    z_in,
    kv,
    bias,
    local_sem,
    x_send,
    x_recv,
    wc_send,
    wc_recv,
    wy_send,
    wy_recv,
    wx_send,
    wx_recv,
    wf_send,
    wf_recv,
    rz_send,
    rz_recv,
    az_send,
    az_recv,
    ay_send,
    ay_recv,
    ac_send,
    ac_recv,
):
    f32, bf16 = jnp.float32, jnp.bfloat16
    me = lax.axis_index("blk")
    core = lax.rem(me, 2)
    chip = me // 2
    y = lax.rem(chip, 2)
    z = chip // 2
    part_index = lax.axis_index("groups")
    shares = 2 if groups % 2 == 0 else 1
    share = lax.rem(part_index, shares)
    depth = n // 4
    levels = depth.bit_length() - 1

    def device(z_, y_, core_):
        return {"blk": (z_ * 2 + y_) * 2 + core_}

    def copy(src, dst, send, recv, z_, y_, core_):
        return pltpu.make_async_remote_copy(
            src_ref=src,
            dst_ref=dst,
            send_sem=send,
            recv_sem=recv,
            device_id=device(z_, y_, core_),
            device_id_type=MESH,
        )

    def other(d):
        v = z
        for j in range(levels):
            if d >> j & 1:
                v = v + 2**j - v // 2**j % 2 * 2 ** (j + 1)
        return v

    zs = [other(d) for d in range(depth)]
    _, rows, features = x_in.shape
    head_dim = q_gain.shape[1]
    w_rows, kv_cols = w_hbm.shape
    kv_width = kv_cols // 2
    kv_heads = kv_width // head_dim
    text_rows = q_hbm.shape[0]
    query_heads = q_hbm.shape[1] // head_dim
    group = query_heads // kv_heads
    keys = n * rows
    pieces = kv.shape[0]
    width = kv_width // pieces
    piece_heads = kv_heads // pieces

    peers = [device(at, y, core) for at in zs[1:]]
    peers += [device(z, 1 - y, core), device(z, y, 1 - core)]
    if shares == 2:
        peers.append({"groups": part_index + 1 - 2 * share, "blk": me})
    barrier = pltpu.get_barrier_semaphore()
    for peer in peers:
        pl.semaphore_signal(barrier, inc=1, device_id=peer, device_id_type=MESH)

    def x_block(pz):
        return x_hbm.at[:, pl.ds(pl.multiple_of(pz * features, features), features)]

    size = w_rows // shares
    steps = wy_send.shape[0]
    w_step = size // steps

    def w_block(y_, share_, i):
        start = (y_ * 2 + core) * w_rows + share_ * size + i * w_step
        return w.at[pl.ds(pl.multiple_of(start, w_step), w_step)]

    own_w = w.at[pl.ds(pl.multiple_of((y * 2 + core) * w_rows, w_rows), w_rows)]
    x_local = pltpu.make_async_copy(x_block(z), x_in.at[z], local_sem.at[0])
    w_local = pltpu.make_async_copy(w_hbm, own_w, local_sem.at[1])
    q_local = pltpu.make_async_copy(q_hbm, q_raw, local_sem.at[2])
    x_local.start()
    w_local.start()
    q_local.start()

    pl.semaphore_wait(barrier, len(peers))

    sent = []

    def send(d):
        d.start()
        sent.append(d)

    def w_y(i):
        start = pl.multiple_of(share * size + i * w_step, w_step)
        source = w_hbm.at[pl.ds(start, w_step)]
        return copy(source, w_block(y, share, i), wy_send.at[i], wy_recv.at[i], z, 1 - y, core)

    def w_x(i, share_):
        block = w_block(1 - y, share_, i)
        return pltpu.make_async_remote_copy(
            src_ref=block,
            dst_ref=block,
            send_sem=wx_send.at[i],
            recv_sem=wx_recv.at[i],
            device_id=peers[-1],
            device_id_type=MESH,
        )

    def w_core(i, a):
        block = w_block(1 - y, share if a == 0 else 1 - share, i)
        return copy(block, block, wf_send.at[a, i], wf_recv.at[a, i], z, y, 1 - core)

    w_c = copy(w_hbm, own_w, wc_send, wc_recv, z, y, 1 - core)

    row_steps, row_step = x_send.shape[0], rows // x_send.shape[0]

    def x_step(r, at):
        some = pl.ds(r * row_step, row_step)
        start = pl.multiple_of(at * features, features)
        return copy(
            x_hbm.at[some, pl.ds(start, features)],
            x_in.at[z, some],
            x_send.at[r, at],
            x_recv.at[r, z],
            at,
            y,
            core,
        )

    def send_x(r):
        if r < row_steps:
            for at in reversed(zs[1:]):
                send(x_step(r, at))

    send(w_y(0))
    send_x(0)
    for i in range(1, steps):
        send(w_y(i))
        if i == 1:
            send(w_c)
            send_x(1)

    def from_y(i):
        w_y(i).wait_recv()
        if shares == 2:
            send(w_x(i, share))
        send(w_core(i, 0))
        if i == 0:
            for r in range(2, row_steps):
                send_x(r)

    def from_x(i):
        if shares == 2:
            w_x(i, 1 - share).wait_recv()
            send(w_core(i, 1))

    q_local.wait()
    for h in range(query_heads):
        v = q_raw[:, h * head_dim : (h + 1) * head_dim].astype(f32)
        mean = jnp.mean(v * v, axis=-1, keepdims=True)
        v = v * lax.rsqrt(mean + epsilon) * q_gain[...]
        at = (h % group) * text_rows
        q_normed[h // group, at : at + text_rows, :] = v.astype(bf16)
        if (h + 1) % (query_heads // (2 * steps)) == 0:
            i = (h + 1) // (query_heads // (2 * steps)) - 1 - steps
            if i >= 0:
                from_y(i)
                if i:
                    from_x(i - 1)
    from_x(steps - 1)

    t_pos = lax.broadcasted_iota(jnp.int32, (text_rows, keys), 0) + me * text_rows
    key = lax.broadcasted_iota(jnp.int32, (1, keys), 1)
    slot = key // rows
    key_device = (slot % depth * 2 + slot // depth % 2) * 2 + slot // (2 * depth)
    p_pos = key_device * rows + key % rows
    segment = jnp.zeros((text_rows, keys), jnp.int32)
    owner = jnp.zeros((1, keys), jnp.int32)
    t_end, p_end = jnp.int32(0), jnp.int32(0)
    for j in range(text_counts.shape[0]):
        t_end = t_end + text_counts[j]
        p_end = p_end + image_counts[j]
        segment = segment + jnp.where(t_pos >= t_end, 1, 0)
        owner = owner + jnp.where(p_pos >= p_end, 1, 0)
    bias[...] = jnp.where(owner <= segment, 0.0, -1e30).astype(f32)

    x_local.wait()
    w_local.wait()
    w_c.wait_recv()
    for i in range(steps):
        for a in range(shares):
            w_core(i, a).wait_recv()

    def z_step(h, at):
        return copy(
            z_out.at[h, at], z_in.at[h, z], rz_send.at[h, at], rz_recv.at[h, z], at, y, core
        )

    def project(slices):
        for at in slices:
            if at is not z:
                for r in range(row_steps):
                    block = x_in.at[at, pl.ds(r * row_step, row_step)]
                    copy(block, block, x_send.at[r, at], x_recv.at[r, at], at, y, core).wait_recv()
        block = jnp.concatenate([x_in[at] for at in slices], axis=0)
        for h in range(pieces):
            for i in range(2):
                cols = slice(i * kv_width + h * width, i * kv_width + (h + 1) * width)
                product = jnp.dot(block, w[:, cols], preferred_element_type=f32)
                cols = slice(i * width, (i + 1) * width)
                for a, at in enumerate(slices):
                    piece = product[a * rows : (a + 1) * rows]
                    if at is z:
                        part[h, :, cols] = piece
                    else:
                        z_out[h, at, :, cols] = piece.astype(bf16)
            for at in slices:
                if at is not z:
                    send(z_step(h, at))

    def finish(h):
        total = part[h]
        for at in zs[1:]:
            block = z_in.at[h, at]
            copy(block, block, rz_send.at[h, at], rz_recv.at[h, at], at, y, core).wait_recv()
            total = total + z_in[h, at].astype(f32)
        for g in range(piece_heads):
            at = slice(g * head_dim, (g + 1) * head_dim)
            v = total[:, at]
            mean = jnp.mean(v * v, axis=-1, keepdims=True)
            kv[h, core, y, z, :, at] = (v * lax.rsqrt(mean + epsilon) * k_gain[...]).astype(bf16)
        kv[h, core, y, z, :, width:] = total[:, width:].astype(bf16)
        own = kv.at[h, core, y, z]
        for at in reversed(zs[1:]):
            send(copy(own, own, az_send.at[h, at], az_recv.at[h, z], at, y, core))
        send(to_y(h, z))

    def to_y(h, at):
        block = kv.at[h, core, y, at]
        return copy(block, block, ay_send.at[h, at], ay_recv.at[h, at], z, 1 - y, core)

    def column(h, core_, y_):
        block = kv.at[h, core_, y_]
        return copy(block, block, ac_send.at[h, y_], ac_recv.at[h, y_], z, y, 1 - core)

    def gather_z(h):
        for at in zs[1:]:
            block = kv.at[h, core, y, at]
            copy(block, block, az_send.at[h, at], az_recv.at[h, at], at, y, core).wait_recv()
            send(to_y(h, at))
        send(column(h, core, y))

    def gather_y(h):
        for at in zs:
            block = kv.at[h, core, 1 - y, at]
            copy(block, block, ay_send.at[h, at], ay_recv.at[h, at], z, 1 - y, core).wait_recv()
        send(column(h, core, 1 - y))

    scale = math.log2(math.e) / math.sqrt(head_dim)
    pair = math.gcd(group, 2)
    tile = pair * text_rows

    def attend(h, i):
        if i == 0:
            for yb in (y, 1 - y):
                column(h, 1 - core, yb).wait_recv()
        g = h * piece_heads + i
        k_at = slice(i * head_dim, (i + 1) * head_dim)
        v_at = slice(width + i * head_dim, width + (i + 1) * head_dim)
        key_block = kv[h, :, :, :, :, k_at].reshape(keys, head_dim)
        value_block = kv[h, :, :, :, :, v_at].reshape(keys, head_dim)
        value_block = jnp.concatenate([value_block, jnp.ones_like(value_block)], axis=1)
        for t in range(group // pair):
            scores = lax.dot_general(
                q_normed[g, t * tile : (t + 1) * tile, :],
                key_block,
                (((1,), (1,)), ((), ())),
                preferred_element_type=f32,
            )
            scores = scores.reshape(pair, text_rows, keys) * scale + bias[...][None]
            weights = jnp.exp2(scores).astype(bf16).reshape(tile, keys)
            total = jnp.dot(weights, value_block, preferred_element_type=f32)
            result = (total[:, :head_dim] / total[:, head_dim:]).astype(bf16)
            for a in range(pair):
                col = (g * group + t * pair + a) * head_dim
                out[:, col : col + head_dim] = result[a * text_rows : (a + 1) * text_rows]

    for d in range(0, depth, 2):
        project(zs[d : d + 2])
    for h in range(pieces):
        finish(h)
    waiting = []
    for h in range(pieces):
        gather_z(h)
        if waiting:
            attend(*waiting.pop(0))
        gather_y(h)
        for p in waiting:
            attend(*p)
        waiting = [(h, i) for i in range(piece_heads)]
    for p in waiting:
        attend(*p)

    for d in sent:
        d.wait_send()


def body(n, groups, text_queries, image_states, kv_weight, q_gain, k_gain, text_counts, image_counts):
    f32, bf16 = jnp.float32, jnp.bfloat16
    rows = image_states.shape[0]
    features = image_states.shape[1] * 4 // n
    w_rows, kv_cols = kv_weight.shape
    text_rows, q_cols = text_queries.shape
    head_dim = q_gain.shape[0]
    kv_heads = kv_cols // 2 // head_dim
    group = q_cols // head_dim // kv_heads
    depth = n // 4
    pieces = math.gcd(kv_heads, 2)
    cols = kv_cols // pieces
    row_steps = rows // 16 if rows % 16 == 0 else 1
    steps = 4 if w_rows % 128 == 0 else 1
    vmem = pl.BlockSpec(memory_space=pltpu.VMEM)
    smem = pl.BlockSpec(memory_space=pltpu.SMEM)
    anywhere = pl.BlockSpec(memory_space=pl.ANY)
    dma = pltpu.SemaphoreType.DMA
    return pl.pallas_call(
        functools.partial(kernel, n, groups),
        out_shape=jax.ShapeDtypeStruct((text_rows, q_cols), bf16),
        in_specs=[anywhere, anywhere, anywhere, vmem, vmem, smem, smem],
        out_specs=vmem,
        scratch_shapes=[
            pltpu.VMEM((text_rows, q_cols), bf16),
            pltpu.VMEM((kv_heads, group * text_rows, head_dim), bf16),
            pltpu.VMEM((depth, rows, features), bf16),
            pltpu.VMEM((4 * w_rows, kv_cols), bf16),
            pltpu.VMEM((pieces, rows, cols), f32),
            pltpu.VMEM((pieces, depth, rows, cols), bf16),
            pltpu.VMEM((pieces, depth, rows, cols), bf16),
            pltpu.VMEM((pieces, 2, 2, depth, rows, cols), bf16),
            pltpu.VMEM((text_rows, n * rows), f32),
            dma((3,)),
            dma((row_steps, depth)),
            dma((row_steps, depth)),
            dma,
            dma,
            dma((steps,)),
            dma((steps,)),
            dma((steps,)),
            dma((steps,)),
            dma((2, steps)),
            dma((2, steps)),
            dma((pieces, depth)),
            dma((pieces, depth)),
            dma((pieces, depth)),
            dma((pieces, depth)),
            dma((pieces, depth)),
            dma((pieces, depth)),
            dma((pieces, 2)),
            dma((pieces, 2)),
        ],
        compiler_params=pltpu.CompilerParams(
            collective_id=0, has_side_effects=True, vmem_limit_bytes=60 << 20
        ),
    )(
        text_queries,
        image_states,
        kv_weight,
        q_gain.reshape(1, head_dim),
        k_gain.reshape(1, head_dim),
        text_counts,
        image_counts,
    )


def solution(mesh):
    placed = (
        P(("groups", "blk"), None),
        P(("groups", "blk"), None),
        P("blk", None),
        P(),
        P(),
        P("groups"),
        P("groups"),
    )
    return jax.shard_map(
        functools.partial(body, mesh.shape["blk"], mesh.shape["groups"]),
        mesh=mesh,
        in_specs=placed,
        out_specs=P(("groups", "blk"), None),
        check_vma=False,
    )
```
